32 devices in a mesh: fsdp: 4 (over x, core), grp: 2 (over y), rep: 4 (over z).
Axes of the slice: x: 2, y: 2, z: 4, core: 2. Of those that a mesh axis runs over, the one named last changes fastest.
Arguments:
- iterate: bfloat16 [4096, 7168], P(('fsdp', 'grp', 'rep')), may hold values from -0.040283203 to 0.040283203
Outputs:
- update: bfloat16 [4096, 7168], P('fsdp', ('grp', 'rep'))
The draws below stay inside these ranges and needn't reach their ends.
All inputs are finite; a program needn't handle non-finite values.
Results may differ from the reference program's by a relative error of at most 0.0059.
Values may be sent and summed in bfloat16 or wider, within the bound.
No kernel may reach another device: no remote copies, remote signals or barrier semaphores. Data moves between devices by JAX's collectives and lax.ppermute only.
A program may use at most 64 MiB of HBM per device.

```python
import math
import jax
import jax.numpy as jnp
from jax import lax

COLS = 7168
ROWS = 4096


def shard_levels(own_key, extent, shards, low, high):
    factor_of = 1.0
    for axis_at, shards_of in shards:
        draws = jax.random.uniform(jax.random.fold_in(jax.random.fold_in(own_key, 6), axis_at), (shards_of,), jnp.float32, low / len(shards), high / len(shards))
        factor_of = factor_of * jnp.repeat(jnp.exp(draws), extent[axis_at] // shards_of).reshape((-1,) + (1,) * (len(extent) - 1 - axis_at))
    return factor_of


def gaussian(stream_key, extent, deviation, bound, pieces=(), kind=jnp.bfloat16):
    drawn = jax.random.normal(stream_key, extent, jnp.float32) * deviation
    if len(pieces) > 0:
        drawn = shard_levels(stream_key, extent, pieces, -0.22, 0.18) * drawn
    return jnp.clip(drawn, min=-bound, max=bound).astype(kind)


def setup_inputs(seed: int = 0) -> dict:
    key_of = jax.random.split(jax.random.key(seed), 2)
    return {
        "iterate": gaussian(key_of[0], (ROWS, COLS), (1 / (ROWS ** 0.5 + COLS ** 0.5)), 0.040283203, ((0, 32),)),
    }


coef_linear = 3.4445
coef_cubic = -4.775
coef_quintic = 2.0315

def reference(iterate):
    gram = lax.dot_general(iterate, iterate, (((1,), (1,)), ((), ())), preferred_element_type=jnp.float32).astype(jnp.bfloat16)
    first = jnp.dot(gram, iterate, preferred_element_type=jnp.float32).astype(jnp.bfloat16)
    second = jnp.dot(gram, first, preferred_element_type=jnp.float32)
    factor = 0.2 * math.sqrt(COLS)
    combined = coef_linear * iterate.astype(jnp.float32) + coef_cubic * first.astype(jnp.float32) + coef_quintic * second
    return (factor * combined).astype(jnp.bfloat16)
```

```python
import math

import jax
import jax.numpy as jnp
from jax import lax
from jax.experimental import pallas as pl
from jax.experimental.layout import Layout, with_layout_constraint
from jax.experimental.pallas import tpu as pltpu
from jax.sharding import PartitionSpec as P

COLS = 7168


coef_linear = 3.4445
coef_cubic = -4.775
coef_quintic = 2.0315


def after(value, *earlier):
    return lax.optimization_barrier((value,) + earlier)[0]


def dot_rows(left, right):
    return lax.dot_general(
        left, right, (((1,), (1,)), ((), ())), preferred_element_type=jnp.float32
    ).astype(jnp.bfloat16)


DEPTH = 1024


def accumulate(left, right, total):
    part = jnp.dot(left[...], right[...], preferred_element_type=jnp.float32)

    @pl.when(pl.program_id(0) == 0)
    def _():
        total[...] = part

    @pl.when(pl.program_id(0) > 0)
    def _():
        total[...] += part


def first_kernel(left, right, out, total):
    accumulate(left, right, total)

    @pl.when(pl.program_id(0) == pl.num_programs(0) - 1)
    def _():
        out[...] = total[...].astype(out.dtype)


def product(left, right, rows, row_at):
    depth, width = right.shape
    step = math.gcd(DEPTH, depth)
    return pl.pallas_call(
        first_kernel,
        out_shape=jax.ShapeDtypeStruct((rows, width), jnp.bfloat16),
        grid=(depth // step,),
        in_specs=[
            pl.BlockSpec((rows, step), lambda at: (row_at, at)),
            pl.BlockSpec((step, width), lambda at: (at, 0)),
        ],
        out_specs=pl.BlockSpec((rows, width), lambda at: (0, 0)),
        scratch_shapes=[pltpu.VMEM((rows, width), jnp.float32)],
        compiler_params=pltpu.CompilerParams(vmem_limit_bytes=48 << 20),
        cost_estimate=pl.CostEstimate(
            flops=2 * rows * depth * width,
            bytes_accessed=2 * (rows * depth + depth * width + rows * width),
            transcendentals=0,
        ),
    )(left, right)


def second_begin_kernel(count):
    def kernel(columns, left, *refs):
        rights, (held, top, bottom, out) = refs[:count], refs[count:]
        factor = 0.2 * math.sqrt(COLS)

        @pl.when(pl.program_id(0) == 0)
        def _():
            half = top.shape[0]
            for at, image in ((0, top), (half, bottom)):
                rows = pl.ds(at, half)
                out[rows, :] = factor * (
                    coef_linear * held[rows, :].astype(jnp.float32)
                    + coef_cubic * image[...].astype(jnp.float32)
                )

        for at, right in enumerate(rights):

            @pl.when(pl.program_id(0) == at)
            def _(right=right):
                part = jnp.dot(left[...], right[...], preferred_element_type=jnp.float32)
                out[...] += (factor * coef_quintic) * part

    return kernel


def second_end_kernel(count):
    def kernel(columns, left, *refs):
        rights, (begun, out, total) = refs[:count], refs[count:]
        factor = 0.2 * math.sqrt(COLS)
        for at, right in enumerate(rights):

            @pl.when(pl.program_id(0) == at)
            def _(at=at, right=right):
                part = jnp.dot(left[...], right[...], preferred_element_type=jnp.float32)
                before = begun if at == 0 else total
                total[...] = before[...] + (factor * coef_quintic) * part

        @pl.when(pl.program_id(0) == count - 1)
        def _():
            out[...] = total[...].astype(out.dtype)

    return kernel


def add_terms(kernel, gram, columns, rights, others, kind, scratch=False):
    rows = gram.shape[0]
    depth, width = rights[0].shape

    def fixed(value):
        return pl.BlockSpec(
            value.shape, lambda at, columns: (0, 0), pipeline_mode=pl.Buffered(1)
        )

    return pl.pallas_call(
        kernel(len(rights)),
        out_shape=jax.ShapeDtypeStruct((rows, width), kind),
        grid_spec=pltpu.PrefetchScalarGridSpec(
            num_scalar_prefetch=1,
            grid=(len(rights),),
            in_specs=[pl.BlockSpec((rows, depth), lambda at, columns: (0, columns[at]))]
            + [fixed(value) for value in (*rights, *others)],
            out_specs=pl.BlockSpec((rows, width), lambda at, columns: (0, 0)),
            scratch_shapes=[pltpu.VMEM((rows, width), jnp.float32)] if scratch else [],
        ),
        compiler_params=pltpu.CompilerParams(vmem_limit_bytes=48 << 20),
        cost_estimate=pl.CostEstimate(
            flops=2 * rows * depth * width * len(rights),
            bytes_accessed=2 * len(rights) * depth * (rows + width) + 8 * rows * width,
            transcendentals=0,
        ),
    )(columns, gram, *rights, *others)


def begin_kernel(side, block, out):
    out[...] = block[...]


def begin_gram(block, side, columns, column_at):
    rows, width = block.shape
    return pl.pallas_call(
        begin_kernel,
        out_shape=jax.ShapeDtypeStruct((2 * rows, columns * width), block.dtype),
        grid_spec=pltpu.PrefetchScalarGridSpec(
            num_scalar_prefetch=1,
            grid=(1,),
            in_specs=[pl.BlockSpec((rows, width), lambda at, side: (0, 0))],
            out_specs=pl.BlockSpec((rows, width), lambda at, side: (side[0], column_at)),
        ),
        cost_estimate=pl.CostEstimate(
            flops=0, bytes_accessed=4 * rows * width, transcendentals=0
        ),
    )(side.reshape(1), block)


def by_rows(value):
    return with_layout_constraint(value, Layout(tuple(range(value.ndim))))


def make_body(n_row, n_grp, n_rep):
    n_chip = n_row // 2
    n_col = n_grp * n_rep
    over = ("grp", "rep")
    swap_cores = [(at, at ^ 1) for at in range(n_row)]

    def from_chip(value, step):
        pairs = [(at, (at - 2 * step) % n_row) for at in range(n_row)]
        return lax.ppermute(value, "fsdp", pairs)

    def on_chip(value):
        return lax.ppermute(value, "fsdp", swap_cores)

    def place(at):
        return (at % n_chip) * 2 + (at % n_row) // n_chip

    def ring(value, step):
        pairs = [(place(at), place(at + step)) for at in range(n_row)]
        return lax.ppermute(value, "fsdp", pairs)

    def begin_sum(value):
        assert n_grp & (n_grp - 1) == 0
        bit = 1
        while True:
            rows = value.shape[0] // 2
            side = (lax.axis_index("grp") // bit) % 2
            kept = lax.dynamic_slice_in_dim(value, side * rows, rows, 0)
            sent = lax.dynamic_slice_in_dim(value, (1 - side) * rows, rows, 0)
            got = lax.ppermute(sent, "grp", [(at, at ^ bit) for at in range(n_grp)])
            if 2 * bit == n_grp:
                return kept, sent, got
            value = (kept.astype(jnp.float32) + got.astype(jnp.float32)).astype(value.dtype)
            bit = 2 * bit

    rep_bits = [1 << at for at in range(n_rep.bit_length() - 1)][::-1]
    grp_bits = [1 << at for at in range(n_grp.bit_length() - 1)][::-1]
    over_rep = [("rep", n_rep, bit) for bit in rep_bits]
    over_grp = [("grp", n_grp, bit) for bit in grp_bits]

    def swap(value, axis, size, bit):
        return lax.ppermute(value, axis, [(at, at ^ bit) for at in range(size)])

    def join(value, got, axis, bit, known_grp, known_rep):
        side = (lax.axis_index(axis) // bit) % 2
        lower = jnp.where(side == 0, value, got)
        upper = jnp.where(side == 0, got, value)
        return jnp.stack([lower, upper], axis=0 if axis == "grp" else known_grp + known_rep)

    class Gather:
        def __init__(self, value, steps):
            self.value, self.steps = value, list(steps)
            self.known = {"grp": 0, "rep": 0}

        def send(self):
            return swap(self.value, *self.steps[0])

        def take(self, got):
            axis, _, bit = self.steps.pop(0)
            self.value = join(
                self.value, got, axis, bit, self.known["grp"], self.known["rep"]
            )
            self.known[axis] += 1

    def cut_sum(parts):
        added = [
            (kept.astype(jnp.float32) + got.astype(jnp.float32))
            .astype(kept.dtype)
            .reshape(n_rep, -1, kept.shape[1])
            for kept, got in parts
        ]
        return jnp.concatenate(added, axis=1)

    def to_rep(cut):
        return lax.all_to_all(cut, "rep", split_axis=0, concat_axis=0, tiled=True)

    def end_sum(pieces):
        return jnp.sum(pieces.astype(jnp.float32), axis=0).astype(pieces.dtype)

    def body(iterate):
        at_row = lax.axis_index("fsdp")
        chip, core = at_row // 2, at_row % 2
        held = lax.all_to_all(iterate, over, split_axis=1, concat_axis=0, tiled=True)
        rows, width = held.shape
        half = rows // 2
        cut_at = rows // n_col
        other = on_chip(held)
        far = [from_chip(held, step) for step in range(1, n_chip)]

        slots = [jnp.int32(0), jnp.int32(1)]
        for step in range(1, n_chip):
            near = chip + step < n_chip
            ahead_slot, behind_slot = 2 * step, 2 * (n_chip - step) + 1
            slots.append(jnp.where(near, ahead_slot, behind_slot))
            slots.append(jnp.where(near, behind_slot, ahead_slot))

        def in_order(found, start=0, whole=None):
            size, width = found[0].shape
            if whole is None:
                whole = jnp.zeros((n_row * rows, width), found[0].dtype)
            for at, block in enumerate(found):
                whole = lax.dynamic_update_slice(whole, block, (slots[at] * rows + start, 0))
            return whole

        kept_own, sent_own, got_own = begin_sum(dot_rows(held, held))
        quadrant_at = core * half
        upper = dot_rows(
            after(held[:half], sent_own), lax.dynamic_slice_in_dim(other, quadrant_at, half, 0)
        )
        right = dot_rows(lax.dynamic_slice_in_dim(held, quadrant_at, half, 0), other[half:])
        kept_pair, _, got_pair = begin_sum(jnp.concatenate([upper, right], axis=1))

        panel, started = [held, other], []
        for step in range(1, n_chip):
            far_own, got_own, got_pair = lax.optimization_barrier(
                (far[step - 1], got_own, got_pair)
            )
            far_other = on_chip(far_own)
            panel += [far_own, far_other]
            right = jnp.where(chip + step < n_chip, far_own, far_other)
            started.append(begin_sum(by_rows(dot_rows(held, right))))
        kept_own = after(kept_own, *[sent for _, sent, _ in started])
        near_pieces = to_rep(cut_sum([(kept_own, got_own), (kept_pair, got_pair)]))
        cut = cut_sum([(kept, got) for kept, _, got in started])
        near_pieces, cut = lax.optimization_barrier((near_pieces, cut))
        near = Gather(end_sum(near_pieces), over_grp)
        while len(near.steps) > 1:
            near.take(near.send())
        near_got = near.send()
        whole = in_order(panel)
        pieces, near_got, whole = lax.optimization_barrier((to_rep(cut), near_got, whole))
        ahead = Gather(end_sum(pieces), over_rep + over_grp[:-1])
        near.take(near_got)
        own = Gather(near.value[..., :cut_at, :], over_rep)
        pair = Gather(near.value[..., cut_at:, :], over_rep)
        own.known["grp"] = pair.known["grp"] = len(over_grp)

        ahead_got = ahead.send()
        ahead.take(ahead_got)
        pair.value = after(pair.value, ahead_got)
        pair_got = pair.send()
        while ahead.steps:
            ahead.take(ahead.send())

        side_here = lax.axis_index("grp") % 2
        here = side_here * half
        there = half - here
        steps = range(1, n_chip)
        own_half = [
            by_rows(ahead.value[..., (at - 1) * cut_at : at * cut_at, :].reshape(half, rows))
            for at in steps
        ]
        def put(block, row, column):
            return lax.dynamic_update_slice(gram_rows, block, (row, column))

        rung_here = [ring(block, at) for at, block in zip(steps, own_half)]
        pair.take(after(pair_got, *own_half))
        while len(pair.steps) > 1:
            pair.take(pair.send())
        own_got, pair_got = own.send(), pair.send()
        came, rung_there = [], []
        for side in range(2):
            columns = [block[:, side * half : (side + 1) * half] for block in own_half]
            if came:
                columns[0] = after(columns[0], *came[0])
            came.append([swap(block, *over_grp[-1]) for block in columns])
            rung_there.append([ring(block, at) for at, block in zip(steps, came[side])])

        gram_rows = begin_gram(own_half[0], side_here, n_row, 2)
        for at, block in zip(steps[1:], own_half[1:]):
            gram_rows = put(block, here, 2 * at * rows)

        def put_came(side):
            (*blocks, held_rows) = lax.optimization_barrier((*came[side], gram_rows))
            for at, block in zip(steps, blocks):
                held_rows = lax.dynamic_update_slice(
                    held_rows, block, (there, 2 * at * rows + side * half)
                )
            return held_rows

        def put_rung(blocks, row, offset):
            (*blocks, held_rows) = lax.optimization_barrier((*blocks, gram_rows))
            for at, block in zip(steps, blocks):
                held_rows = lax.dynamic_update_slice(
                    held_rows, block.T, (row, (2 * at + 1) * rows + offset)
                )
            return held_rows

        gram_rows = put_came(0)
        pair_got, gram_rows = lax.optimization_barrier((pair_got, gram_rows))
        pair.take(pair_got)
        pair_half = pair.value.reshape(half, rows)
        pair_other = on_chip(pair_half)
        gram_rows = put(pair_half[:, :half], 0, rows + quadrant_at)
        gram_rows = put(pair_half[:, half:], quadrant_at, rows + half)
        own_got, gram_rows = lax.optimization_barrier((own_got, gram_rows))
        own.take(own_got)
        while len(own.steps) > 1:
            own.take(own.send())
        own_got = own.send()
        gram_rows, _ = lax.optimization_barrier((gram_rows, own.value))
        gram_rows = put_rung(rung_here, 0, here)
        gram_rows = put_came(1)
        gram_rows = put_rung(rung_there[0], 0, there)
        pair_other, gram_rows = lax.optimization_barrier((pair_other, gram_rows))
        gram_rows = put(pair_other[:, :half].T, half - quadrant_at, rows)
        gram_rows = put(pair_other[:, half:].T, half, rows + half - quadrant_at)
        own_got, gram_rows = lax.optimization_barrier((own_got, gram_rows))
        own.take(own_got)
        gram_rows = put(own.value.reshape(rows, rows), 0, 0)
        images = [product(gram_rows, whole, half, 0)]
        gram_rows = after(gram_rows, images[0])
        gram_rows = put_rung(rung_there[1], half, there)
        images.append(product(gram_rows, whole, half, 1))

        def spread(image, *earlier):
            found = [image, on_chip(image)]
            for step in range(1, n_chip):
                got = from_chip(image, step)
                if earlier:
                    got = after(got, *earlier)
                found += [got, on_chip(got)]
            return found

        top = spread(images[0], images[1])
        if half % 128 == 0:
            other = on_chip(images[1])
            early = [*top, images[1], other]
            columns = [2 * slot for slot in slots] + [jnp.int32(1), jnp.int32(3)]
            begun = add_terms(
                second_begin_kernel,
                gram_rows,
                jnp.stack(columns),
                early,
                (held, *images),
                jnp.float32,
            )
            late = []
            for step in range(1, n_chip):
                got = after(from_chip(images[1], step), begun)
                late += [got, on_chip(got)]
            columns = jnp.stack([2 * slot + 1 for slot in slots[2:]])
            return add_terms(
                second_end_kernel, gram_rows, columns, late, (begun,), jnp.bfloat16, True
            )

        bottom = spread(images[1])
        spread_image = in_order(bottom, half, in_order(top))
        second_image = jnp.dot(gram_rows, spread_image, preferred_element_type=jnp.float32)
        image = jnp.concatenate(images, axis=0)
        factor = 0.2 * math.sqrt(COLS)
        combined = (
            coef_linear * held.astype(jnp.float32)
            + coef_cubic * image.astype(jnp.float32)
            + coef_quintic * second_image
        )
        return (factor * combined).astype(jnp.bfloat16)

    return body


def solution(mesh):
    sizes = mesh.shape
    in_specs = (P(("fsdp", "grp", "rep"), None),)
    out_specs = P("fsdp", ("grp", "rep"))
    body = make_body(sizes["fsdp"], sizes["grp"], sizes["rep"])
    return jax.shard_map(body, mesh=mesh, in_specs=in_specs, out_specs=out_specs, check_vma=False)
```

```python
import math

import jax
import jax.numpy as jnp
from jax import lax
from jax.experimental import pallas as pl
from jax.experimental.layout import Layout, with_layout_constraint
from jax.experimental.pallas import tpu as pltpu
from jax.sharding import PartitionSpec as P

COLS = 7168


coef_linear = 3.4445
coef_cubic = -4.775
coef_quintic = 2.0315


def after(value, *earlier):
    return lax.optimization_barrier((value,) + earlier)[0]


def dot_rows(left, right):
    return lax.dot_general(
        left, right, (((1,), (1,)), ((), ())), preferred_element_type=jnp.float32
    ).astype(jnp.bfloat16)


DEPTH = 1024


def accumulate(left, right, total):
    part = jnp.dot(left[...], right[...], preferred_element_type=jnp.float32)

    @pl.when(pl.program_id(0) == 0)
    def _():
        total[...] = part

    @pl.when(pl.program_id(0) > 0)
    def _():
        total[...] += part


def first_kernel(left, right, out, total):
    accumulate(left, right, total)

    @pl.when(pl.program_id(0) == pl.num_programs(0) - 1)
    def _():
        out[...] = total[...].astype(out.dtype)


def product(left, right, rows, row_at):
    depth, width = right.shape
    step = math.gcd(DEPTH, depth)
    return pl.pallas_call(
        first_kernel,
        out_shape=jax.ShapeDtypeStruct((rows, width), jnp.bfloat16),
        grid=(depth // step,),
        in_specs=[
            pl.BlockSpec((rows, step), lambda at: (row_at, at)),
            pl.BlockSpec((step, width), lambda at: (at, 0)),
        ],
        out_specs=pl.BlockSpec((rows, width), lambda at: (0, 0)),
        scratch_shapes=[pltpu.VMEM((rows, width), jnp.float32)],
        compiler_params=pltpu.CompilerParams(vmem_limit_bytes=48 << 20),
        cost_estimate=pl.CostEstimate(
            flops=2 * rows * depth * width,
            bytes_accessed=2 * (rows * depth + depth * width + rows * width),
            transcendentals=0,
        ),
    )(left, right)


def second_begin_kernel(count):
    def kernel(columns, left, *refs):
        rights, (held, top, bottom, out) = refs[:count], refs[count:]
        factor = 0.2 * math.sqrt(COLS)

        @pl.when(pl.program_id(0) == 0)
        def _():
            half = top.shape[0]
            for at, image in ((0, top), (half, bottom)):
                rows = pl.ds(at, half)
                out[rows, :] = factor * (
                    coef_linear * held[rows, :].astype(jnp.float32)
                    + coef_cubic * image[...].astype(jnp.float32)
                )

        for at, right in enumerate(rights):

            @pl.when(pl.program_id(0) == at)
            def _(right=right):
                part = jnp.dot(left[...], right[...], preferred_element_type=jnp.float32)
                out[...] += (factor * coef_quintic) * part

    return kernel


def second_end_kernel(count):
    def kernel(columns, left, *refs):
        rights, (begun, out, total) = refs[:count], refs[count:]
        factor = 0.2 * math.sqrt(COLS)
        for at, right in enumerate(rights):

            @pl.when(pl.program_id(0) == at)
            def _(at=at, right=right):
                part = jnp.dot(left[...], right[...], preferred_element_type=jnp.float32)
                before = begun if at == 0 else total
                total[...] = before[...] + (factor * coef_quintic) * part

        @pl.when(pl.program_id(0) == count - 1)
        def _():
            out[...] = total[...].astype(out.dtype)

    return kernel


def add_terms(kernel, gram, columns, rights, others, kind, scratch=False, limit=48 << 20):
    rows = gram.shape[0]
    depth, width = rights[0].shape

    def fixed(value):
        return pl.BlockSpec(
            value.shape, lambda at, columns: (0, 0), pipeline_mode=pl.Buffered(1)
        )

    return pl.pallas_call(
        kernel(len(rights)),
        out_shape=jax.ShapeDtypeStruct((rows, width), kind),
        grid_spec=pltpu.PrefetchScalarGridSpec(
            num_scalar_prefetch=1,
            grid=(len(rights),),
            in_specs=[pl.BlockSpec((rows, depth), lambda at, columns: (0, columns[at]))]
            + [fixed(value) for value in (*rights, *others)],
            out_specs=pl.BlockSpec((rows, width), lambda at, columns: (0, 0)),
            scratch_shapes=[pltpu.VMEM((rows, width), jnp.float32)] if scratch else [],
        ),
        compiler_params=pltpu.CompilerParams(vmem_limit_bytes=limit),
        cost_estimate=pl.CostEstimate(
            flops=2 * rows * depth * width * len(rights),
            bytes_accessed=2 * len(rights) * depth * (rows + width) + 8 * rows * width,
            transcendentals=0,
        ),
    )(columns, gram, *rights, *others)


def begin_kernel(side, block, out):
    out[...] = block[...]


def begin_gram(block, side, columns, column_at):
    rows, width = block.shape
    return pl.pallas_call(
        begin_kernel,
        out_shape=jax.ShapeDtypeStruct((2 * rows, columns * width), block.dtype),
        grid_spec=pltpu.PrefetchScalarGridSpec(
            num_scalar_prefetch=1,
            grid=(1,),
            in_specs=[pl.BlockSpec((rows, width), lambda at, side: (0, 0))],
            out_specs=pl.BlockSpec((rows, width), lambda at, side: (side[0], column_at)),
        ),
        cost_estimate=pl.CostEstimate(
            flops=0, bytes_accessed=4 * rows * width, transcendentals=0
        ),
    )(side.reshape(1), block)


def by_rows(value):
    return with_layout_constraint(value, Layout(tuple(range(value.ndim))))


def make_body(n_row, n_grp, n_rep):
    n_chip = n_row // 2
    n_col = n_grp * n_rep
    over = ("grp", "rep")
    swap_cores = [(at, at ^ 1) for at in range(n_row)]

    def from_chip(value, step):
        pairs = [(at, (at - 2 * step) % n_row) for at in range(n_row)]
        return lax.ppermute(value, "fsdp", pairs)

    def on_chip(value):
        return lax.ppermute(value, "fsdp", swap_cores)

    def place(at):
        return (at % n_chip) * 2 + (at % n_row) // n_chip

    def ring(value, step):
        pairs = [(place(at), place(at + step)) for at in range(n_row)]
        return lax.ppermute(value, "fsdp", pairs)

    def begin_sum(value):
        assert n_grp & (n_grp - 1) == 0
        bit = 1
        while True:
            rows = value.shape[0] // 2
            side = (lax.axis_index("grp") // bit) % 2
            kept = lax.dynamic_slice_in_dim(value, side * rows, rows, 0)
            sent = lax.dynamic_slice_in_dim(value, (1 - side) * rows, rows, 0)
            got = lax.ppermute(sent, "grp", [(at, at ^ bit) for at in range(n_grp)])
            if 2 * bit == n_grp:
                return kept, sent, got
            value = (kept.astype(jnp.float32) + got.astype(jnp.float32)).astype(value.dtype)
            bit = 2 * bit

    rep_bits = [1 << at for at in range(n_rep.bit_length() - 1)][::-1]
    grp_bits = [1 << at for at in range(n_grp.bit_length() - 1)][::-1]
    over_rep = [("rep", n_rep, bit) for bit in rep_bits]
    over_grp = [("grp", n_grp, bit) for bit in grp_bits]

    def swap(value, axis, size, bit):
        return lax.ppermute(value, axis, [(at, at ^ bit) for at in range(size)])

    def join(value, got, axis, bit, known_grp, known_rep):
        side = (lax.axis_index(axis) // bit) % 2
        lower = jnp.where(side == 0, value, got)
        upper = jnp.where(side == 0, got, value)
        return jnp.stack([lower, upper], axis=0 if axis == "grp" else known_grp + known_rep)

    class Gather:
        def __init__(self, value, steps):
            self.value, self.steps = value, list(steps)
            self.known = {"grp": 0, "rep": 0}

        def send(self):
            return swap(self.value, *self.steps[0])

        def take(self, got):
            axis, _, bit = self.steps.pop(0)
            self.value = join(
                self.value, got, axis, bit, self.known["grp"], self.known["rep"]
            )
            self.known[axis] += 1

    def cut_sum(parts):
        added = [
            (kept.astype(jnp.float32) + got.astype(jnp.float32))
            .astype(kept.dtype)
            .reshape(n_rep, -1, kept.shape[1])
            for kept, got in parts
        ]
        return jnp.concatenate(added, axis=1)

    def to_rep(cut):
        return lax.all_to_all(cut, "rep", split_axis=0, concat_axis=0, tiled=True)

    def end_sum(pieces):
        return jnp.sum(pieces.astype(jnp.float32), axis=0).astype(pieces.dtype)

    def body(iterate):
        at_row = lax.axis_index("fsdp")
        chip, core = at_row // 2, at_row % 2
        held = lax.all_to_all(iterate, over, split_axis=1, concat_axis=0, tiled=True)
        rows, width = held.shape
        half = rows // 2
        cut_at = rows // n_col
        other = on_chip(held)
        far = [from_chip(held, step) for step in range(1, n_chip)]

        slots = [jnp.int32(0), jnp.int32(1)]
        for step in range(1, n_chip):
            near = chip + step < n_chip
            ahead_slot, behind_slot = 2 * step, 2 * (n_chip - step) + 1
            slots.append(jnp.where(near, ahead_slot, behind_slot))
            slots.append(jnp.where(near, behind_slot, ahead_slot))

        def in_order(found, start=0, whole=None):
            size, width = found[0].shape
            if whole is None:
                whole = jnp.zeros((n_row * rows, width), found[0].dtype)
            for at, block in enumerate(found):
                whole = lax.dynamic_update_slice(whole, block, (slots[at] * rows + start, 0))
            return whole

        kept_own, sent_own, got_own = begin_sum(dot_rows(held, held))
        quadrant_at = core * half
        upper = dot_rows(
            after(held[:half], sent_own), lax.dynamic_slice_in_dim(other, quadrant_at, half, 0)
        )
        right = dot_rows(lax.dynamic_slice_in_dim(held, quadrant_at, half, 0), other[half:])
        kept_pair, _, got_pair = begin_sum(jnp.concatenate([upper, right], axis=1))

        panel, started = [held, other], []
        for step in range(1, n_chip):
            far_own, got_own, got_pair = lax.optimization_barrier(
                (far[step - 1], got_own, got_pair)
            )
            far_other = on_chip(far_own)
            panel += [far_own, far_other]
            right = jnp.where(chip + step < n_chip, far_own, far_other)
            started.append(begin_sum(by_rows(dot_rows(held, right))))
        near_pieces = to_rep(cut_sum([(kept_own, got_own), (kept_pair, got_pair)]))
        cut = cut_sum([(kept, got) for kept, _, got in started])
        near_pieces, cut = lax.optimization_barrier((near_pieces, cut))
        near_piece = end_sum(near_pieces)
        own = Gather(near_piece[:cut_at], over_rep + over_grp[:-1])
        pair = Gather(near_piece[cut_at:], over_grp + over_rep)
        while len(pair.steps) > len(over_rep) + 1:
            pair.take(pair.send())
        pair_got = pair.send()
        whole = in_order(panel)
        pieces, pair_got, whole = lax.optimization_barrier((to_rep(cut), pair_got, whole))
        ahead = Gather(end_sum(pieces), over_rep + over_grp[:-1])
        pair.take(pair_got)

        ahead_got = ahead.send()
        ahead.take(ahead_got)
        pair.value = after(pair.value, ahead_got)
        pair_got = pair.send()
        while ahead.steps:
            ahead.take(ahead.send())

        side_here = lax.axis_index("grp") % 2
        here = side_here * half
        there = half - here
        steps = range(1, n_chip)
        own_half = [
            by_rows(ahead.value[..., (at - 1) * cut_at : at * cut_at, :].reshape(half, rows))
            for at in steps
        ]
        def put(block, row, column):
            return lax.dynamic_update_slice(gram_rows, block, (row, column))

        rung_here = [ring(block, at) for at, block in zip(steps, own_half)]
        pair.take(after(pair_got, *own_half))
        while len(pair.steps) > 1:
            pair.take(pair.send())
        own.value = after(own.value, *own_half)
        own_got, pair_got = own.send(), pair.send()
        came, rung_there = [], []
        for side in range(2):
            columns = [block[:, side * half : (side + 1) * half] for block in own_half]
            if came:
                columns[0] = after(columns[0], *came[0])
            came.append([swap(block, *over_grp[-1]) for block in columns])
            rung_there.append([ring(block, at) for at, block in zip(steps, came[side])])

        gram_rows = begin_gram(own_half[0], side_here, n_row, 2)
        for at, block in zip(steps[1:], own_half[1:]):
            gram_rows = put(block, here, 2 * at * rows)

        def put_came(side):
            (*blocks, held_rows) = lax.optimization_barrier((*came[side], gram_rows))
            for at, block in zip(steps, blocks):
                held_rows = lax.dynamic_update_slice(
                    held_rows, block, (there, 2 * at * rows + side * half)
                )
            return held_rows

        def put_rung(blocks, row, offset):
            (*blocks, held_rows) = lax.optimization_barrier((*blocks, gram_rows))
            for at, block in zip(steps, blocks):
                held_rows = lax.dynamic_update_slice(
                    held_rows, block.T, (row, (2 * at + 1) * rows + offset)
                )
            return held_rows

        gram_rows = put_came(0)
        pair_got, gram_rows = lax.optimization_barrier((pair_got, gram_rows))
        pair.take(pair_got)
        pair_half = pair.value.reshape(half, rows)
        pair_other = on_chip(pair_half)
        gram_rows = put(pair_half[:, :half], 0, rows + quadrant_at)
        gram_rows = put(pair_half[:, half:], quadrant_at, rows + half)
        own_got, gram_rows = lax.optimization_barrier((own_got, gram_rows))
        own.take(own_got)
        while len(own.steps) > 1:
            own.take(own.send())
        own_got = own.send()
        gram_rows, _ = lax.optimization_barrier((gram_rows, own.value))
        gram_rows = put_came(1)
        gram_rows = put_rung(rung_here, 0, here)
        own_got, gram_rows = lax.optimization_barrier((own_got, gram_rows))
        own.take(own_got)
        own_rows = own.value.reshape(half, rows)
        own_came = swap(own_rows, *over_grp[-1])
        gram_rows = put(own_rows, here, 0)
        gram_rows = put_rung(rung_there[0], 0, there)
        pair_other, gram_rows = lax.optimization_barrier((pair_other, gram_rows))
        gram_rows = put(pair_other[:, :half].T, half - quadrant_at, rows)
        gram_rows = put(pair_other[:, half:].T, half, rows + half - quadrant_at)
        own_came, gram_rows = lax.optimization_barrier((own_came, gram_rows))
        gram_rows = put(own_came, there, 0)
        images = [product(gram_rows, whole, half, 0)]
        gram_rows = after(gram_rows, images[0])
        gram_rows = put_rung(rung_there[1], half, there)
        images.append(product(gram_rows, whole, half, 1))

        def spread(image, *earlier):
            found = [image, on_chip(image)]
            for step in range(1, n_chip):
                got = from_chip(image, step)
                if earlier:
                    got = after(got, *earlier)
                found += [got, on_chip(got)]
            return found

        top = spread(images[0], images[1])
        if half % 128 == 0:
            other = on_chip(images[1])
            early = [*top, images[1], other]
            columns = [2 * slot for slot in slots] + [jnp.int32(1), jnp.int32(3)]
            begun = add_terms(
                second_begin_kernel,
                gram_rows,
                jnp.stack(columns),
                early,
                (held, *images),
                jnp.float32,
            )
            late = []
            for step in range(1, n_chip):
                got = after(from_chip(images[1], step), begun)
                late += [got, on_chip(got)]
            columns = jnp.stack([2 * slot + 1 for slot in slots[2:]])
            return add_terms(
                second_end_kernel,
                gram_rows,
                columns,
                late,
                (begun,),
                jnp.bfloat16,
                scratch=True,
                limit=58 << 20,
            )

        bottom = spread(images[1])
        spread_image = in_order(bottom, half, in_order(top))
        second_image = jnp.dot(gram_rows, spread_image, preferred_element_type=jnp.float32)
        image = jnp.concatenate(images, axis=0)
        factor = 0.2 * math.sqrt(COLS)
        combined = (
            coef_linear * held.astype(jnp.float32)
            + coef_cubic * image.astype(jnp.float32)
            + coef_quintic * second_image
        )
        return (factor * combined).astype(jnp.bfloat16)

    return body


def solution(mesh):
    sizes = mesh.shape
    in_specs = (P(("fsdp", "grp", "rep"), None),)
    out_specs = P("fsdp", ("grp", "rep"))
    body = make_body(sizes["fsdp"], sizes["grp"], sizes["rep"])
    return jax.shard_map(body, mesh=mesh, in_specs=in_specs, out_specs=out_specs, check_vma=False)
```

```python
import math

import jax
import jax.numpy as jnp
from jax import lax
from jax.experimental import pallas as pl
from jax.experimental.layout import Layout, with_layout_constraint
from jax.experimental.pallas import tpu as pltpu
from jax.sharding import PartitionSpec as P

COLS = 7168


coef_linear = 3.4445
coef_cubic = -4.775
coef_quintic = 2.0315


def after(value, *earlier):
    return lax.optimization_barrier((value,) + earlier)[0]


def dot_rows(left, right):
    return lax.dot_general(
        left, right, (((1,), (1,)), ((), ())), preferred_element_type=jnp.float32
    ).astype(jnp.bfloat16)


DEPTH = 1024


def accumulate(left, right, total):
    part = jnp.dot(left[...], right[...], preferred_element_type=jnp.float32)

    @pl.when(pl.program_id(0) == 0)
    def _():
        total[...] = part

    @pl.when(pl.program_id(0) > 0)
    def _():
        total[...] += part


def first_kernel(left, right, out, total):
    accumulate(left, right, total)

    @pl.when(pl.program_id(0) == pl.num_programs(0) - 1)
    def _():
        out[...] = total[...].astype(out.dtype)


def product(left, right, rows, row_at):
    depth, width = right.shape
    step = math.gcd(DEPTH, depth)
    return pl.pallas_call(
        first_kernel,
        out_shape=jax.ShapeDtypeStruct((rows, width), jnp.bfloat16),
        grid=(depth // step,),
        in_specs=[
            pl.BlockSpec((rows, step), lambda at: (row_at, at)),
            pl.BlockSpec((step, width), lambda at: (at, 0)),
        ],
        out_specs=pl.BlockSpec((rows, width), lambda at: (0, 0)),
        scratch_shapes=[pltpu.VMEM((rows, width), jnp.float32)],
        compiler_params=pltpu.CompilerParams(vmem_limit_bytes=48 << 20),
    )(left, right)


def second_begin_kernel(count):
    def kernel(columns, left, *refs):
        rights, (held, image_here, image_there, out) = refs[:count], refs[count:]
        factor = 0.2 * math.sqrt(COLS)

        @pl.when(pl.program_id(0) == 0)
        def _():
            half = image_here.shape[0]
            side = columns[count]
            for at, row_half, image in ((0, side, image_here), (half, 1 - side, image_there)):
                held_rows = held[pl.ds(pl.multiple_of(row_half * half, half), half), :]
                out[pl.ds(at, half), :] = factor * (
                    coef_linear * held_rows.astype(jnp.float32)
                    + coef_cubic * image[...].astype(jnp.float32)
                )

        for at, right in enumerate(rights):

            @pl.when(pl.program_id(0) == at)
            def _(right=right):
                part = jnp.dot(left[...], right[...], preferred_element_type=jnp.float32)
                out[...] += (factor * coef_quintic) * part

    return kernel


def second_end_kernel(count):
    def kernel(columns, left, *refs):
        rights, (begun, out, total) = refs[:count], refs[count:]
        factor = 0.2 * math.sqrt(COLS)
        for at, right in enumerate(rights):

            @pl.when(pl.program_id(0) == at)
            def _(at=at, right=right):
                part = jnp.dot(left[...], right[...], preferred_element_type=jnp.float32)
                before = begun if at == 0 else total
                total[...] = before[...] + (factor * coef_quintic) * part

        @pl.when(pl.program_id(0) == count - 1)
        def _():
            half = total.shape[0] // 2
            side = columns[count]
            for at, row_half in ((0, side), (half, 1 - side)):
                rows = pl.ds(pl.multiple_of(row_half * half, half), half)
                out[rows, :] = total[pl.ds(at, half), :].astype(out.dtype)

    return kernel


def add_terms(kernel, gram, columns, rights, others, kind, scratch=False, limit=48 << 20):
    rows = gram.shape[0]
    depth, width = rights[0].shape

    def fixed(value):
        return pl.BlockSpec(
            value.shape, lambda at, columns: (0, 0), pipeline_mode=pl.Buffered(1)
        )

    return pl.pallas_call(
        kernel(len(rights)),
        out_shape=jax.ShapeDtypeStruct((rows, width), kind),
        grid_spec=pltpu.PrefetchScalarGridSpec(
            num_scalar_prefetch=1,
            grid=(len(rights),),
            in_specs=[pl.BlockSpec((rows, depth), lambda at, columns: (0, columns[at]))]
            + [fixed(value) for value in (*rights, *others)],
            out_specs=pl.BlockSpec((rows, width), lambda at, columns: (0, 0)),
            scratch_shapes=[pltpu.VMEM((rows, width), jnp.float32)] if scratch else [],
        ),
        compiler_params=pltpu.CompilerParams(vmem_limit_bytes=limit),
    )(columns, gram, *rights, *others)


def begin_kernel(block, out):
    out[...] = block[...]


def begin_gram(block, columns, column_at):
    rows, width = block.shape
    return pl.pallas_call(
        begin_kernel,
        out_shape=jax.ShapeDtypeStruct((2 * rows, columns * width), block.dtype),
        grid=(1,),
        in_specs=[pl.BlockSpec((rows, width), lambda at: (0, 0))],
        out_specs=pl.BlockSpec((rows, width), lambda at: (0, column_at)),
    )(block)


def by_rows(value):
    return with_layout_constraint(value, Layout(tuple(range(value.ndim))))


def make_body(n_row, n_grp, n_rep):
    n_chip = n_row // 2
    n_col = n_grp * n_rep
    over = ("grp", "rep")
    swap_cores = [(at, at ^ 1) for at in range(n_row)]

    def from_chip(value, step):
        pairs = [(at, (at - 2 * step) % n_row) for at in range(n_row)]
        return lax.ppermute(value, "fsdp", pairs)

    def on_chip(value):
        return lax.ppermute(value, "fsdp", swap_cores)

    def place(at):
        return (at % n_chip) * 2 + (at % n_row) // n_chip

    def ring(value, step):
        pairs = [(place(at), place(at + step)) for at in range(n_row)]
        return lax.ppermute(value, "fsdp", pairs)

    def begin_sum(value):
        assert n_grp & (n_grp - 1) == 0
        bit = 1
        while True:
            rows = value.shape[0] // 2
            side = (lax.axis_index("grp") // bit) % 2
            kept = lax.dynamic_slice_in_dim(value, side * rows, rows, 0)
            sent = lax.dynamic_slice_in_dim(value, (1 - side) * rows, rows, 0)
            got = lax.ppermute(sent, "grp", [(at, at ^ bit) for at in range(n_grp)])
            if 2 * bit == n_grp:
                return kept, sent, got
            value = (kept.astype(jnp.float32) + got.astype(jnp.float32)).astype(value.dtype)
            bit = 2 * bit

    rep_bits = [1 << at for at in range(n_rep.bit_length() - 1)][::-1]
    grp_bits = [1 << at for at in range(n_grp.bit_length() - 1)][::-1]
    over_rep = [("rep", n_rep, bit) for bit in rep_bits]
    over_grp = [("grp", n_grp, bit) for bit in grp_bits]

    def swap(value, axis, size, bit):
        return lax.ppermute(value, axis, [(at, at ^ bit) for at in range(size)])

    def join(value, got, axis, bit, known_grp, known_rep):
        side = (lax.axis_index(axis) // bit) % 2
        lower = jnp.where(side == 0, value, got)
        upper = jnp.where(side == 0, got, value)
        return jnp.stack([lower, upper], axis=0 if axis == "grp" else known_grp + known_rep)

    class Gather:
        def __init__(self, value, steps):
            self.value, self.steps = value, list(steps)
            self.known = {"grp": 0, "rep": 0}

        def send(self):
            return swap(self.value, *self.steps[0])

        def take(self, got):
            axis, _, bit = self.steps.pop(0)
            self.value = join(
                self.value, got, axis, bit, self.known["grp"], self.known["rep"]
            )
            self.known[axis] += 1

    def cut_sum(parts):
        added = [
            (kept.astype(jnp.float32) + got.astype(jnp.float32))
            .astype(kept.dtype)
            .reshape(n_rep, -1, kept.shape[1])
            for kept, got in parts
        ]
        return jnp.concatenate(added, axis=1)

    def to_rep(cut):
        return lax.all_to_all(cut, "rep", split_axis=0, concat_axis=0, tiled=True)

    def end_sum(pieces):
        return jnp.sum(pieces.astype(jnp.float32), axis=0).astype(pieces.dtype)

    def body(iterate):
        at_row = lax.axis_index("fsdp")
        chip, core = at_row // 2, at_row % 2
        held = lax.all_to_all(iterate, over, split_axis=1, concat_axis=0, tiled=True)
        rows, width = held.shape
        half = rows // 2
        cut_at = rows // n_col
        other = on_chip(held)
        far = [from_chip(held, step) for step in range(1, n_chip)]

        slots = [jnp.int32(0), jnp.int32(1)]
        for step in range(1, n_chip):
            near = chip + step < n_chip
            ahead_slot, behind_slot = 2 * step, 2 * (n_chip - step) + 1
            slots.append(jnp.where(near, ahead_slot, behind_slot))
            slots.append(jnp.where(near, behind_slot, ahead_slot))

        def in_order(found, start=0, whole=None):
            size, width = found[0].shape
            if whole is None:
                whole = jnp.zeros((n_row * rows, width), found[0].dtype)
            for at, block in enumerate(found):
                whole = lax.dynamic_update_slice(whole, block, (slots[at] * rows + start, 0))
            return whole

        kept_own, sent_own, got_own = begin_sum(dot_rows(held, held))
        quadrant_at = core * half
        upper = dot_rows(
            after(held[:half], sent_own), lax.dynamic_slice_in_dim(other, quadrant_at, half, 0)
        )
        right = dot_rows(lax.dynamic_slice_in_dim(held, quadrant_at, half, 0), other[half:])
        kept_pair, _, got_pair = begin_sum(jnp.concatenate([upper, right], axis=1))

        panel, started = [held, other], []
        for step in range(1, n_chip):
            far_own, got_own, got_pair = lax.optimization_barrier(
                (far[step - 1], got_own, got_pair)
            )
            far_other = on_chip(far_own)
            panel += [far_own, far_other]
            right = jnp.where(chip + step < n_chip, far_own, far_other)
            started.append(begin_sum(by_rows(dot_rows(held, right))))
        near_pieces = to_rep(cut_sum([(kept_own, got_own), (kept_pair, got_pair)]))
        cut = cut_sum([(kept, got) for kept, _, got in started])
        near_pieces, cut = lax.optimization_barrier((near_pieces, cut))
        near_piece = end_sum(near_pieces)
        own = Gather(near_piece[:cut_at], over_rep + over_grp[:-1])
        pair = Gather(near_piece[cut_at:], over_grp + over_rep)
        while len(pair.steps) > len(over_rep) + 1:
            pair.take(pair.send())
        pair_got = pair.send()
        whole = in_order(panel)
        pieces, pair_got, whole = lax.optimization_barrier((to_rep(cut), pair_got, whole))
        ahead = Gather(end_sum(pieces), over_rep + over_grp[:-1])
        pair.take(pair_got)

        ahead_got = ahead.send()
        ahead.take(ahead_got)
        pair.value, own.value, _ = lax.optimization_barrier((pair.value, own.value, ahead_got))
        own_got, pair_got = own.send(), pair.send()
        while ahead.steps:
            ahead.take(ahead.send())

        side_here = lax.axis_index("grp") % 2
        here = side_here * half
        there = half - here
        steps = range(1, n_chip)
        own_half = [
            by_rows(ahead.value[..., (at - 1) * cut_at : at * cut_at, :].reshape(half, rows))
            for at in steps
        ]
        def put(block, row, column):
            return lax.dynamic_update_slice(gram_rows, block, (row, column))

        rung_here = [ring(block, at) for at, block in zip(steps, own_half)]
        own_got, pair_got, *own_half = lax.optimization_barrier((own_got, pair_got, *own_half))
        own.take(own_got)
        pair.take(pair_got)
        while len(own.steps) > 1:
            own.take(own.send())
        while len(pair.steps) > 1:
            pair.take(pair.send())
        own_got = own.send()
        pair.value = after(pair.value, own.value)
        pair_got = pair.send()
        came, rung_there = [], []

        for start in (there, here):
            columns = [lax.dynamic_slice_in_dim(block, start, half, 1) for block in own_half]
            if came:
                columns[0] = after(columns[0], *came[0])
            came.append([swap(block, *over_grp[-1]) for block in columns])
            rung_there.append([ring(block, at) for at, block in zip(steps, came[-1])])

        gram_rows = begin_gram(own_half[0], n_row, 2)
        for at, block in zip(steps[1:], own_half[1:]):
            gram_rows = put(block, 0, 2 * at * rows)

        def put_came(which, column):
            (*blocks, held_rows) = lax.optimization_barrier((*came[which], gram_rows))
            for at, block in zip(steps, blocks):
                held_rows = lax.dynamic_update_slice(
                    held_rows, block, (half, 2 * at * rows + column)
                )
            return held_rows

        def put_rung(blocks, row, column, part=None):
            (*blocks, held_rows) = lax.optimization_barrier((*blocks, gram_rows))
            for at, block in zip(steps, blocks):
                if part is not None:
                    block = lax.dynamic_slice_in_dim(block, part, half, 1)
                held_rows = lax.dynamic_update_slice(
                    held_rows, block.T, (row, (2 * at + 1) * rows + column)
                )
            return held_rows

        gram_rows = put_came(0, here)
        own_got, gram_rows = lax.optimization_barrier((own_got, gram_rows))
        own.take(own_got)
        own_rows = own.value.reshape(half, rows)
        own_came = swap(after(own_rows, *came[1]), *over_grp[-1])
        gram_rows = put(own_rows, 0, 0)
        pair_got, gram_rows = lax.optimization_barrier((pair_got, gram_rows))
        pair.take(pair_got)
        pair_half = pair.value.reshape(half, rows)
        pair_other = on_chip(pair_half)
        gram_rows = put_came(1, there)
        gram_rows = put_rung(rung_here, 0, here, here)
        gram_rows = put_rung(rung_there[0], 0, there)
        pair_other, gram_rows = lax.optimization_barrier((pair_other, gram_rows))

        left, right = pair_half[:, :half], pair_half[:, half:]
        left_t, right_t = pair_other[:, :half].T, pair_other[:, half:].T
        as_first, as_upper = core == 0, side_here == 0

        def put_pair(row, upper):
            first = jnp.where(
                as_first, jnp.where(upper, left, left_t), jnp.where(upper, left_t, right_t)
            )
            second = jnp.where(
                as_first, jnp.where(upper, right, right_t), jnp.where(upper, left, right)
            )
            held_rows = lax.dynamic_update_slice(gram_rows, first, (row, rows))
            return lax.dynamic_update_slice(held_rows, second, (row, rows + half))

        gram_rows = put_pair(0, as_upper)
        images = [product(gram_rows, whole, half, 0)]
        gram_rows = after(gram_rows, images[0])
        gram_rows = put_pair(half, jnp.logical_not(as_upper))
        gram_rows = put_rung(rung_here, half, here, there)
        gram_rows = put_rung(rung_there[1], half, there)
        own_came, gram_rows = lax.optimization_barrier((own_came, gram_rows))
        gram_rows = put(own_came, half, 0)
        images.append(product(gram_rows, whole, half, 1))

        def spread(image, *earlier):
            found = [image, on_chip(image)]
            for step in range(1, n_chip):
                got = from_chip(image, step)
                if earlier:
                    got = after(got, *earlier)
                found += [got, on_chip(got)]
            return found

        found_here = spread(images[0], images[1])
        side_there = 1 - side_here
        if half % 128 == 0:
            early = [*found_here, images[1], on_chip(images[1])]
            columns = [2 * slot + side_here for slot in slots]
            columns += [side_there, 2 + side_there, side_here]
            begun = add_terms(
                second_begin_kernel,
                gram_rows,
                jnp.stack(columns),
                early,
                (held, *images),
                jnp.float32,
            )
            late = []
            for step in range(1, n_chip):
                got = after(from_chip(images[1], step), begun)
                late += [got, on_chip(got)]
            columns = [2 * slot + side_there for slot in slots[2:]] + [side_here]
            return add_terms(
                second_end_kernel,
                gram_rows,
                jnp.stack(columns),
                late,
                (begun,),
                jnp.bfloat16,
                scratch=True,
                limit=58 << 20,
            )

        spread_image = in_order(spread(images[1]), there, in_order(found_here, here))
        second_image = jnp.dot(gram_rows, spread_image, preferred_element_type=jnp.float32)
        factor = 0.2 * math.sqrt(COLS)
        update = jnp.zeros(held.shape, jnp.bfloat16)
        for at, start in enumerate((here, there)):
            combined = (
                coef_linear * lax.dynamic_slice_in_dim(held, start, half, 0).astype(jnp.float32)
                + coef_cubic * images[at].astype(jnp.float32)
                + coef_quintic * second_image[at * half : (at + 1) * half]
            )
            update = lax.dynamic_update_slice_in_dim(
                update, (factor * combined).astype(jnp.bfloat16), start, 0
            )
        return update

    return body


def solution(mesh):
    sizes = mesh.shape
    in_specs = (P(("fsdp", "grp", "rep"), None),)
    out_specs = P("fsdp", ("grp", "rep"))
    body = make_body(sizes["fsdp"], sizes["grp"], sizes["rep"])
    return jax.shard_map(body, mesh=mesh, in_specs=in_specs, out_specs=out_specs, check_vma=False)
```

```python
import math

import jax
import jax.numpy as jnp
from jax import lax
from jax.experimental import pallas as pl
from jax.experimental.layout import Layout, with_layout_constraint
from jax.experimental.pallas import tpu as pltpu
from jax.sharding import PartitionSpec as P

COLS = 7168


coef_linear = 3.4445
coef_cubic = -4.775
coef_quintic = 2.0315


def after(value, *earlier):
    return lax.optimization_barrier((value,) + earlier)[0]


def dot_rows(left, right):
    return lax.dot_general(
        left, right, (((1,), (1,)), ((), ())), preferred_element_type=jnp.float32
    ).astype(jnp.bfloat16)


DEPTH = 1024


def accumulate(left, right, total):
    part = jnp.dot(left[...], right[...], preferred_element_type=jnp.float32)

    @pl.when(pl.program_id(0) == 0)
    def _():
        total[...] = part

    @pl.when(pl.program_id(0) > 0)
    def _():
        total[...] += part


def first_kernel(left, right, out, total):
    accumulate(left, right, total)

    @pl.when(pl.program_id(0) == pl.num_programs(0) - 1)
    def _():
        out[...] = total[...].astype(out.dtype)


def product(left, right, rows, row_at):
    depth, width = right.shape
    step = math.gcd(DEPTH, depth)
    return pl.pallas_call(
        first_kernel,
        out_shape=jax.ShapeDtypeStruct((rows, width), jnp.bfloat16),
        grid=(depth // step,),
        in_specs=[
            pl.BlockSpec((rows, step), lambda at: (row_at, at)),
            pl.BlockSpec((step, width), lambda at: (at, 0)),
        ],
        out_specs=pl.BlockSpec((rows, width), lambda at: (0, 0)),
        scratch_shapes=[pltpu.VMEM((rows, width), jnp.float32)],
        compiler_params=pltpu.CompilerParams(vmem_limit_bytes=48 << 20),
    )(left, right)


def second_begin_kernel(count):
    def kernel(columns, left, *refs):
        rights, (held, image_here, image_there, out) = refs[:count], refs[count:]
        factor = 0.2 * math.sqrt(COLS)

        @pl.when(pl.program_id(0) == 0)
        def _():
            half = image_here.shape[0]
            side = columns[count]
            for at, row_half, image in ((0, side, image_here), (half, 1 - side, image_there)):
                held_rows = held[pl.ds(pl.multiple_of(row_half * half, half), half), :]
                out[pl.ds(at, half), :] = factor * (
                    coef_linear * held_rows.astype(jnp.float32)
                    + coef_cubic * image[...].astype(jnp.float32)
                )

        for at, right in enumerate(rights):

            @pl.when(pl.program_id(0) == at)
            def _(right=right):
                part = jnp.dot(left[...], right[...], preferred_element_type=jnp.float32)
                out[...] += (factor * coef_quintic) * part

    return kernel


def second_end_kernel(count):
    def kernel(columns, left, *refs):
        rights, (begun, out, total) = refs[:count], refs[count:]
        factor = 0.2 * math.sqrt(COLS)
        for at, right in enumerate(rights):

            @pl.when(pl.program_id(0) == at)
            def _(at=at, right=right):
                part = jnp.dot(left[...], right[...], preferred_element_type=jnp.float32)
                before = begun if at == 0 else total
                total[...] = before[...] + (factor * coef_quintic) * part

        @pl.when(pl.program_id(0) == count - 1)
        def _():
            half = total.shape[0] // 2
            side = columns[count]
            for at, row_half in ((0, side), (half, 1 - side)):
                rows = pl.ds(pl.multiple_of(row_half * half, half), half)
                out[rows, :] = total[pl.ds(at, half), :].astype(out.dtype)

    return kernel


def add_terms(kernel, gram, columns, rights, others, kind, scratch=False, limit=48 << 20):
    rows = gram.shape[0]
    depth, width = rights[0].shape

    def fixed(value):
        return pl.BlockSpec(
            value.shape, lambda at, columns: (0, 0), pipeline_mode=pl.Buffered(1)
        )

    return pl.pallas_call(
        kernel(len(rights)),
        out_shape=jax.ShapeDtypeStruct((rows, width), kind),
        grid_spec=pltpu.PrefetchScalarGridSpec(
            num_scalar_prefetch=1,
            grid=(len(rights),),
            in_specs=[pl.BlockSpec((rows, depth), lambda at, columns: (0, columns[at]))]
            + [fixed(value) for value in (*rights, *others)],
            out_specs=pl.BlockSpec((rows, width), lambda at, columns: (0, 0)),
            scratch_shapes=[pltpu.VMEM((rows, width), jnp.float32)] if scratch else [],
        ),
        compiler_params=pltpu.CompilerParams(vmem_limit_bytes=limit),
    )(columns, gram, *rights, *others)


def begin_kernel(block, out):
    out[...] = block[...]


def begin_gram(block, columns, column_at):
    rows, width = block.shape
    return pl.pallas_call(
        begin_kernel,
        out_shape=jax.ShapeDtypeStruct((2 * rows, columns * width), block.dtype),
        grid=(1,),
        in_specs=[pl.BlockSpec((rows, width), lambda at: (0, 0))],
        out_specs=pl.BlockSpec((rows, width), lambda at: (0, column_at)),
    )(block)


def by_rows(value):
    return with_layout_constraint(value, Layout(tuple(range(value.ndim))))


def make_body(n_row, n_grp, n_rep):
    n_chip = n_row // 2
    n_col = n_grp * n_rep
    over = ("grp", "rep")
    swap_cores = [(at, at ^ 1) for at in range(n_row)]

    def from_chip(value, step):
        pairs = [(at, (at - 2 * step) % n_row) for at in range(n_row)]
        return lax.ppermute(value, "fsdp", pairs)

    def on_chip(value):
        return lax.ppermute(value, "fsdp", swap_cores)

    def place(at):
        return (at % n_chip) * 2 + (at % n_row) // n_chip

    def ring(value, step):
        pairs = [(place(at), place(at + step)) for at in range(n_row)]
        return lax.ppermute(value, "fsdp", pairs)

    def begin_sum(value):
        assert n_grp & (n_grp - 1) == 0
        bit = 1
        while True:
            rows = value.shape[0] // 2
            side = (lax.axis_index("grp") // bit) % 2
            kept = lax.dynamic_slice_in_dim(value, side * rows, rows, 0)
            sent = lax.dynamic_slice_in_dim(value, (1 - side) * rows, rows, 0)
            got = lax.ppermute(sent, "grp", [(at, at ^ bit) for at in range(n_grp)])
            if 2 * bit == n_grp:
                return kept, sent, got
            value = (kept.astype(jnp.float32) + got.astype(jnp.float32)).astype(value.dtype)
            bit = 2 * bit

    rep_bits = [1 << at for at in range(n_rep.bit_length() - 1)][::-1]
    grp_bits = [1 << at for at in range(n_grp.bit_length() - 1)][::-1]
    over_rep = [("rep", n_rep, bit) for bit in rep_bits]
    over_grp = [("grp", n_grp, bit) for bit in grp_bits]

    def swap(value, axis, size, bit):
        return lax.ppermute(value, axis, [(at, at ^ bit) for at in range(size)])

    def join(value, got, axis, bit, known_grp, known_rep):
        side = (lax.axis_index(axis) // bit) % 2
        lower = jnp.where(side == 0, value, got)
        upper = jnp.where(side == 0, got, value)
        return jnp.stack([lower, upper], axis=0 if axis == "grp" else known_grp + known_rep)

    class Gather:
        def __init__(self, value, steps):
            self.value, self.steps = value, list(steps)
            self.known = {"grp": 0, "rep": 0}

        def send(self):
            return swap(self.value, *self.steps[0])

        def take(self, got):
            axis, _, bit = self.steps.pop(0)
            self.value = join(
                self.value, got, axis, bit, self.known["grp"], self.known["rep"]
            )
            self.known[axis] += 1

    def cut_sum(parts):
        added = [
            (kept.astype(jnp.float32) + got.astype(jnp.float32))
            .astype(kept.dtype)
            .reshape(n_rep, -1, kept.shape[1])
            for kept, got in parts
        ]
        return jnp.concatenate(added, axis=1)

    def to_rep(cut):
        return lax.all_to_all(cut, "rep", split_axis=0, concat_axis=0, tiled=True)

    def end_sum(pieces):
        return jnp.sum(pieces.astype(jnp.float32), axis=0).astype(pieces.dtype)

    def body(iterate):
        at_row = lax.axis_index("fsdp")
        chip, core = at_row // 2, at_row % 2
        held = lax.all_to_all(iterate, over, split_axis=1, concat_axis=0, tiled=True)
        rows, width = held.shape
        half = rows // 2
        cut_at = rows // n_col
        other = on_chip(held)
        far = [from_chip(held, step) for step in range(1, n_chip)]

        slots = [jnp.int32(0), jnp.int32(1)]
        for step in range(1, n_chip):
            near = chip + step < n_chip
            ahead_slot, behind_slot = 2 * step, 2 * (n_chip - step) + 1
            slots.append(jnp.where(near, ahead_slot, behind_slot))
            slots.append(jnp.where(near, behind_slot, ahead_slot))

        def in_order(found, start=0, whole=None):
            size, width = found[0].shape
            if whole is None:
                whole = jnp.zeros((n_row * rows, width), found[0].dtype)
            for at, block in enumerate(found):
                whole = lax.dynamic_update_slice(whole, block, (slots[at] * rows + start, 0))
            return whole

        kept_own, sent_own, got_own = begin_sum(dot_rows(held, held))
        quadrant_at = core * half
        upper = dot_rows(
            after(held[:half], sent_own), lax.dynamic_slice_in_dim(other, quadrant_at, half, 0)
        )
        right = dot_rows(lax.dynamic_slice_in_dim(held, quadrant_at, half, 0), other[half:])
        kept_pair, _, got_pair = begin_sum(jnp.concatenate([upper, right], axis=1))

        panel, started = [held, other], []
        for step in range(1, n_chip):
            far_own, got_own, got_pair = lax.optimization_barrier(
                (far[step - 1], got_own, got_pair)
            )
            far_other = on_chip(far_own)
            panel += [far_own, far_other]
            right = jnp.where(chip + step < n_chip, far_own, far_other)
            started.append(begin_sum(by_rows(dot_rows(held, right))))
        near_pieces = to_rep(cut_sum([(kept_own, got_own), (kept_pair, got_pair)]))
        cut = cut_sum([(kept, got) for kept, _, got in started])
        near_pieces, cut = lax.optimization_barrier((near_pieces, cut))
        near_piece = end_sum(near_pieces)
        own = Gather(near_piece[:cut_at], over_rep + over_grp[:-1])
        pair = Gather(near_piece[cut_at:], over_grp + over_rep)
        while len(pair.steps) > len(over_rep) + 1:
            pair.take(pair.send())
        pair_got = pair.send()
        whole = in_order(panel)
        pieces, pair_got, whole = lax.optimization_barrier((to_rep(cut), pair_got, whole))
        ahead = Gather(end_sum(pieces), over_rep + over_grp[:-1])
        pair.take(pair_got)

        ahead_got = ahead.send()
        ahead.take(ahead_got)
        pair.value = after(pair.value, ahead_got)
        pair_got = pair.send()
        while ahead.steps:
            ahead.take(ahead.send())

        side_here = lax.axis_index("grp") % 2
        here = side_here * half
        there = half - here
        steps = range(1, n_chip)
        own_half = [
            by_rows(ahead.value[..., (at - 1) * cut_at : at * cut_at, :].reshape(half, rows))
            for at in steps
        ]
        def put(block, row, column):
            return lax.dynamic_update_slice(gram_rows, block, (row, column))

        def columns_from(start):
            return [lax.dynamic_slice_in_dim(block, start, half, 1) for block in own_half]

        def ring_all(blocks):
            return [ring(block, at) for at, block in zip(steps, blocks)]

        def swap_all(blocks):
            return [swap(block, *over_grp[-1]) for block in blocks]

        came_first = swap_all(columns_from(there))
        rung_own = ring_all(columns_from(here))
        pair_got, *own_half = lax.optimization_barrier((pair_got, *own_half))
        pair.take(pair_got)
        while len(pair.steps) > 1:
            pair.take(pair.send())
        pair_got = pair.send()
        own.value = after(own.value, *own_half)
        own_got = own.send()
        rung_first = ring_all(came_first)
        later = columns_from(here)
        later[0] = after(later[0], *came_first)
        came_second = swap_all(later)
        later = columns_from(there)
        later[0] = after(later[0], *rung_own)
        rung_other = ring_all(later)
        rung_second = ring_all(came_second)

        gram_rows = begin_gram(own_half[0], n_row, 2)
        for at, block in zip(steps[1:], own_half[1:]):
            gram_rows = put(block, 0, 2 * at * rows)

        def put_came(blocks, column):
            (*blocks, held_rows) = lax.optimization_barrier((*blocks, gram_rows))
            for at, block in zip(steps, blocks):
                held_rows = lax.dynamic_update_slice(
                    held_rows, block, (half, 2 * at * rows + column)
                )
            return held_rows

        def put_rung(blocks, row, column):
            (*blocks, held_rows) = lax.optimization_barrier((*blocks, gram_rows))
            for at, block in zip(steps, blocks):
                held_rows = lax.dynamic_update_slice(
                    held_rows, block.T, (row, (2 * at + 1) * rows + column)
                )
            return held_rows

        gram_rows = after(gram_rows, *came_first)
        pair_got, gram_rows = lax.optimization_barrier((pair_got, gram_rows))
        pair.take(pair_got)
        pair_half = pair.value.reshape(half, rows)
        pair_other = on_chip(pair_half)
        gram_rows = put_rung(rung_own, 0, here)
        own_got, gram_rows = lax.optimization_barrier((own_got, gram_rows))
        own.take(own_got)
        while len(own.steps) > 1:
            own.take(own.send())
        own_got = own.send()
        gram_rows = after(gram_rows, own.value, *came_second)
        gram_rows = put_rung(rung_first, 0, there)
        pair_other, gram_rows = lax.optimization_barrier((pair_other, gram_rows))

        left, right = pair_half[:, :half], pair_half[:, half:]
        left_t, right_t = pair_other[:, :half].T, pair_other[:, half:].T
        as_first, as_upper = core == 0, side_here == 0

        def put_pair(row, upper):
            first = jnp.where(
                as_first, jnp.where(upper, left, left_t), jnp.where(upper, left_t, right_t)
            )
            second = jnp.where(
                as_first, jnp.where(upper, right, right_t), jnp.where(upper, left, right)
            )
            held_rows = lax.dynamic_update_slice(gram_rows, first, (row, rows))
            return lax.dynamic_update_slice(held_rows, second, (row, rows + half))

        gram_rows = put_pair(0, as_upper)
        own_got, gram_rows = lax.optimization_barrier((own_got, gram_rows))
        own.take(own_got)
        own_rows = own.value.reshape(half, rows)
        own_came = swap(own_rows, *over_grp[-1])
        gram_rows = put(own_rows, 0, 0)
        images = [product(gram_rows, whole, half, 0)]
        gram_rows = after(gram_rows, images[0])
        gram_rows = put_rung(rung_other, half, here)
        gram_rows = put_pair(half, jnp.logical_not(as_upper))
        gram_rows = put_came(came_first, here)
        gram_rows = put_came(came_second, there)
        gram_rows = put_rung(rung_second, half, there)
        own_came, gram_rows = lax.optimization_barrier((own_came, gram_rows))
        gram_rows = put(own_came, half, 0)
        images.append(product(gram_rows, whole, half, 1))

        def spread(image, *earlier):
            found = [image, on_chip(image)]
            for step in range(1, n_chip):
                got = from_chip(image, step)
                if earlier:
                    got = after(got, *earlier)
                found += [got, on_chip(got)]
            return found

        found_here = spread(images[0], images[1])
        side_there = 1 - side_here
        if half % 128 == 0:
            early = [*found_here, images[1], on_chip(images[1])]
            columns = [2 * slot + side_here for slot in slots]
            columns += [side_there, 2 + side_there, side_here]
            begun = add_terms(
                second_begin_kernel,
                gram_rows,
                jnp.stack(columns),
                early,
                (held, *images),
                jnp.float32,
            )
            late = []
            for step in range(1, n_chip):
                got = after(from_chip(images[1], step), begun)
                late += [got, on_chip(got)]
            columns = [2 * slot + side_there for slot in slots[2:]] + [side_here]
            return add_terms(
                second_end_kernel,
                gram_rows,
                jnp.stack(columns),
                late,
                (begun,),
                jnp.bfloat16,
                scratch=True,
                limit=58 << 20,
            )

        spread_image = in_order(spread(images[1]), there, in_order(found_here, here))
        second_image = jnp.dot(gram_rows, spread_image, preferred_element_type=jnp.float32)
        factor = 0.2 * math.sqrt(COLS)
        update = jnp.zeros(held.shape, jnp.bfloat16)
        for at, start in enumerate((here, there)):
            combined = (
                coef_linear * lax.dynamic_slice_in_dim(held, start, half, 0).astype(jnp.float32)
                + coef_cubic * images[at].astype(jnp.float32)
                + coef_quintic * second_image[at * half : (at + 1) * half]
            )
            update = lax.dynamic_update_slice_in_dim(
                update, (factor * combined).astype(jnp.bfloat16), start, 0
            )
        return update

    return body


def solution(mesh):
    sizes = mesh.shape
    in_specs = (P(("fsdp", "grp", "rep"), None),)
    out_specs = P("fsdp", ("grp", "rep"))
    body = make_body(sizes["fsdp"], sizes["grp"], sizes["rep"])
    return jax.shard_map(body, mesh=mesh, in_specs=in_specs, out_specs=out_specs, check_vma=False)
```

```python
import math

import jax
import jax.numpy as jnp
from jax import lax
from jax.experimental import pallas as pl
from jax.experimental.layout import Layout, with_layout_constraint
from jax.experimental.pallas import tpu as pltpu
from jax.sharding import PartitionSpec as P

COLS = 7168


coef_linear = 3.4445
coef_cubic = -4.775
coef_quintic = 2.0315


def after(value, *earlier):
    return lax.optimization_barrier((value,) + earlier)[0]


def dot_rows(left, right):
    return lax.dot_general(
        left, right, (((1,), (1,)), ((), ())), preferred_element_type=jnp.float32
    ).astype(jnp.bfloat16)


DEPTH = 1024


def accumulate(left, right, total):
    part = jnp.dot(left[...], right[...], preferred_element_type=jnp.float32)

    @pl.when(pl.program_id(0) == 0)
    def _():
        total[...] = part

    @pl.when(pl.program_id(0) > 0)
    def _():
        total[...] += part


def first_kernel(left, right, out, total):
    accumulate(left, right, total)

    @pl.when(pl.program_id(0) == pl.num_programs(0) - 1)
    def _():
        out[...] = total[...].astype(out.dtype)


def product(left, right, rows, row_at):
    depth, width = right.shape
    step = math.gcd(DEPTH, depth)
    return pl.pallas_call(
        first_kernel,
        out_shape=jax.ShapeDtypeStruct((rows, width), jnp.bfloat16),
        grid=(depth // step,),
        in_specs=[
            pl.BlockSpec((rows, step), lambda at: (row_at, at)),
            pl.BlockSpec((step, width), lambda at: (at, 0)),
        ],
        out_specs=pl.BlockSpec((rows, width), lambda at: (0, 0)),
        scratch_shapes=[pltpu.VMEM((rows, width), jnp.float32)],
        compiler_params=pltpu.CompilerParams(vmem_limit_bytes=48 << 20),
    )(left, right)


def second_begin_kernel(count):
    def kernel(columns, left, *refs):
        rights, (held, image_here, image_there, out) = refs[:count], refs[count:]
        factor = 0.2 * math.sqrt(COLS)

        @pl.when(pl.program_id(0) == 0)
        def _():
            half = image_here.shape[0]
            side = columns[count]
            for at, row_half, image in ((0, side, image_here), (half, 1 - side, image_there)):
                held_rows = held[pl.ds(pl.multiple_of(row_half * half, half), half), :]
                out[pl.ds(at, half), :] = factor * (
                    coef_linear * held_rows.astype(jnp.float32)
                    + coef_cubic * image[...].astype(jnp.float32)
                )

        for at, right in enumerate(rights):

            @pl.when(pl.program_id(0) == at)
            def _(right=right):
                part = jnp.dot(left[...], right[...], preferred_element_type=jnp.float32)
                out[...] += (factor * coef_quintic) * part

    return kernel


def second_end_kernel(count):
    def kernel(columns, left, *refs):
        rights, (begun, out, total) = refs[:count], refs[count:]
        factor = 0.2 * math.sqrt(COLS)
        for at, right in enumerate(rights):

            @pl.when(pl.program_id(0) == at)
            def _(at=at, right=right):
                part = jnp.dot(left[...], right[...], preferred_element_type=jnp.float32)
                before = begun if at == 0 else total
                total[...] = before[...] + (factor * coef_quintic) * part

        @pl.when(pl.program_id(0) == count - 1)
        def _():
            half = total.shape[0] // 2
            side = columns[count]
            for at, row_half in ((0, side), (half, 1 - side)):
                rows = pl.ds(pl.multiple_of(row_half * half, half), half)
                out[rows, :] = total[pl.ds(at, half), :].astype(out.dtype)

    return kernel


def add_terms(kernel, gram, columns, rights, others, kind, scratch=False, limit=48 << 20):
    rows = gram.shape[0]
    depth, width = rights[0].shape

    def fixed(value):
        return pl.BlockSpec(
            value.shape, lambda at, columns: (0, 0), pipeline_mode=pl.Buffered(1)
        )

    return pl.pallas_call(
        kernel(len(rights)),
        out_shape=jax.ShapeDtypeStruct((rows, width), kind),
        grid_spec=pltpu.PrefetchScalarGridSpec(
            num_scalar_prefetch=1,
            grid=(len(rights),),
            in_specs=[pl.BlockSpec((rows, depth), lambda at, columns: (0, columns[at]))]
            + [fixed(value) for value in (*rights, *others)],
            out_specs=pl.BlockSpec((rows, width), lambda at, columns: (0, 0)),
            scratch_shapes=[pltpu.VMEM((rows, width), jnp.float32)] if scratch else [],
        ),
        compiler_params=pltpu.CompilerParams(vmem_limit_bytes=limit),
    )(columns, gram, *rights, *others)


def begin_kernel(block, out):
    out[...] = block[...]


def begin_gram(block, columns, column_at):
    rows, width = block.shape
    return pl.pallas_call(
        begin_kernel,
        out_shape=jax.ShapeDtypeStruct((2 * rows, columns * width), block.dtype),
        grid=(1,),
        in_specs=[pl.BlockSpec((rows, width), lambda at: (0, 0))],
        out_specs=pl.BlockSpec((rows, width), lambda at: (0, column_at)),
    )(block)


def by_rows(value):
    return with_layout_constraint(value, Layout(tuple(range(value.ndim))))


def make_body(n_row, n_grp, n_rep):
    n_chip = n_row // 2
    n_col = n_grp * n_rep
    over = ("grp", "rep")
    swap_cores = [(at, at ^ 1) for at in range(n_row)]

    def from_chip(value, step):
        pairs = [(at, (at - 2 * step) % n_row) for at in range(n_row)]
        return lax.ppermute(value, "fsdp", pairs)

    def on_chip(value):
        return lax.ppermute(value, "fsdp", swap_cores)

    def place(at):
        return (at % n_chip) * 2 + (at % n_row) // n_chip

    def ring(value, step):
        pairs = [(place(at), place(at + step)) for at in range(n_row)]
        return lax.ppermute(value, "fsdp", pairs)

    def begin_sum(value):
        assert n_grp & (n_grp - 1) == 0
        bit = 1
        while True:
            rows = value.shape[0] // 2
            side = (lax.axis_index("grp") // bit) % 2
            kept = lax.dynamic_slice_in_dim(value, side * rows, rows, 0)
            sent = lax.dynamic_slice_in_dim(value, (1 - side) * rows, rows, 0)
            got = lax.ppermute(sent, "grp", [(at, at ^ bit) for at in range(n_grp)])
            if 2 * bit == n_grp:
                return kept, sent, got
            value = (kept.astype(jnp.float32) + got.astype(jnp.float32)).astype(value.dtype)
            bit = 2 * bit

    rep_bits = [1 << at for at in range(n_rep.bit_length() - 1)][::-1]
    grp_bits = [1 << at for at in range(n_grp.bit_length() - 1)][::-1]
    over_rep = [("rep", n_rep, bit) for bit in rep_bits]
    over_grp = [("grp", n_grp, bit) for bit in grp_bits]

    def swap(value, axis, size, bit):
        return lax.ppermute(value, axis, [(at, at ^ bit) for at in range(size)])

    def join(value, got, axis, bit, known_grp, known_rep):
        side = (lax.axis_index(axis) // bit) % 2
        lower = jnp.where(side == 0, value, got)
        upper = jnp.where(side == 0, got, value)
        return jnp.stack([lower, upper], axis=0 if axis == "grp" else known_grp + known_rep)

    class Gather:
        def __init__(self, value, steps):
            self.value, self.steps = value, list(steps)
            self.known = {"grp": 0, "rep": 0}

        def send(self):
            return swap(self.value, *self.steps[0])

        def take(self, got):
            axis, _, bit = self.steps.pop(0)
            self.value = join(
                self.value, got, axis, bit, self.known["grp"], self.known["rep"]
            )
            self.known[axis] += 1

    def cut_sum(parts):
        added = [
            (kept.astype(jnp.float32) + got.astype(jnp.float32))
            .astype(kept.dtype)
            .reshape(n_rep, -1, kept.shape[1])
            for kept, got in parts
        ]
        return jnp.concatenate(added, axis=1)

    def to_rep(cut):
        return lax.all_to_all(cut, "rep", split_axis=0, concat_axis=0, tiled=True)

    def end_sum(pieces):
        return jnp.sum(pieces.astype(jnp.float32), axis=0).astype(pieces.dtype)

    def body(iterate):
        at_row = lax.axis_index("fsdp")
        chip, core = at_row // 2, at_row % 2
        held = lax.all_to_all(iterate, over, split_axis=1, concat_axis=0, tiled=True)
        rows, width = held.shape
        half = rows // 2
        cut_at = rows // n_col
        other = on_chip(held)
        far = [from_chip(held, step) for step in range(1, n_chip)]

        slots = [jnp.int32(0), jnp.int32(1)]
        for step in range(1, n_chip):
            near = chip + step < n_chip
            ahead_slot, behind_slot = 2 * step, 2 * (n_chip - step) + 1
            slots.append(jnp.where(near, ahead_slot, behind_slot))
            slots.append(jnp.where(near, behind_slot, ahead_slot))

        def in_order(found, start=0, whole=None):
            size, width = found[0].shape
            if whole is None:
                whole = jnp.zeros((n_row * rows, width), found[0].dtype)
            for at, block in enumerate(found):
                whole = lax.dynamic_update_slice(whole, block, (slots[at] * rows + start, 0))
            return whole

        kept_own, sent_own, got_own = begin_sum(dot_rows(held, held))
        quadrant_at = core * half
        upper = dot_rows(
            after(held[:half], sent_own), lax.dynamic_slice_in_dim(other, quadrant_at, half, 0)
        )
        right = dot_rows(lax.dynamic_slice_in_dim(held, quadrant_at, half, 0), other[half:])
        kept_pair, _, got_pair = begin_sum(jnp.concatenate([upper, right], axis=1))

        panel, started = [held, other], []
        for step in range(1, n_chip):
            far_own, got_own, got_pair = lax.optimization_barrier(
                (far[step - 1], got_own, got_pair)
            )
            far_other = on_chip(far_own)
            panel += [far_own, far_other]
            right = jnp.where(chip + step < n_chip, far_own, far_other)
            started.append(begin_sum(by_rows(dot_rows(held, right))))
        near_pieces = to_rep(cut_sum([(kept_own, got_own), (kept_pair, got_pair)]))
        cut = cut_sum([(kept, got) for kept, _, got in started])
        near_pieces, cut = lax.optimization_barrier((near_pieces, cut))
        near_piece = end_sum(near_pieces)
        own = Gather(near_piece[:cut_at], over_rep + over_grp[:-1])
        pair = Gather(near_piece[cut_at:], over_grp + over_rep)
        while len(pair.steps) > len(over_rep) + 1:
            pair.take(pair.send())
        pair_got = pair.send()
        whole = in_order(panel)
        pieces, pair_got, whole = lax.optimization_barrier((to_rep(cut), pair_got, whole))
        ahead = Gather(end_sum(pieces), over_rep + over_grp[:-1])
        pair.take(pair_got)

        ahead_got = ahead.send()
        ahead.take(ahead_got)
        pair.value = after(pair.value, ahead_got)
        pair_got = pair.send()
        while ahead.steps:
            ahead.take(ahead.send())

        side_here = lax.axis_index("grp") % 2
        here = side_here * half
        there = half - here
        steps = range(1, n_chip)
        own_half = [
            by_rows(ahead.value[..., (at - 1) * cut_at : at * cut_at, :].reshape(half, rows))
            for at in steps
        ]
        def put(block, row, column):
            return lax.dynamic_update_slice(gram_rows, block, (row, column))

        def columns_from(start):
            return [lax.dynamic_slice_in_dim(block, start, half, 1) for block in own_half]

        def ring_all(blocks):
            return [ring(block, at) for at, block in zip(steps, blocks)]

        def swap_all(blocks):
            return [swap(block, *over_grp[-1]) for block in blocks]

        came_first = swap_all(columns_from(there))
        rung_own = ring_all(own_half)
        pair_got, *own_half = lax.optimization_barrier((pair_got, *own_half))
        pair.take(pair_got)
        while len(pair.steps) > 1:
            pair.take(pair.send())
        pair_got = pair.send()
        own.value = after(own.value, *own_half)
        own_got = own.send()
        rung_first = ring_all(came_first)
        later = columns_from(here)
        later[0] = after(later[0], *came_first)
        came_second = swap_all(later)
        rung_second = ring_all(came_second)

        gram_rows = begin_gram(own_half[0], n_row, 2)
        for at, block in zip(steps[1:], own_half[1:]):
            gram_rows = put(block, 0, 2 * at * rows)

        def put_came(blocks, column):
            (*blocks, held_rows) = lax.optimization_barrier((*blocks, gram_rows))
            for at, block in zip(steps, blocks):
                held_rows = lax.dynamic_update_slice(
                    held_rows, block, (half, 2 * at * rows + column)
                )
            return held_rows

        def put_rung(blocks, row, column, part=None):
            (*blocks, held_rows) = lax.optimization_barrier((*blocks, gram_rows))
            for at, block in zip(steps, blocks):
                if part is not None:
                    block = lax.dynamic_slice_in_dim(block, part, half, 1)
                held_rows = lax.dynamic_update_slice(
                    held_rows, block.T, (row, (2 * at + 1) * rows + column)
                )
            return held_rows

        gram_rows = after(gram_rows, *came_first)
        pair_got, gram_rows = lax.optimization_barrier((pair_got, gram_rows))
        pair.take(pair_got)
        pair_half = pair.value.reshape(half, rows)
        pair_other = on_chip(pair_half)
        own_got, gram_rows = lax.optimization_barrier((own_got, gram_rows))
        own.take(own_got)
        while len(own.steps) > 1:
            own.take(own.send())
        own_got = own.send()
        gram_rows = after(gram_rows, own.value, *came_second)
        gram_rows = put_rung(rung_own, 0, here, here)
        pair_other, gram_rows = lax.optimization_barrier((pair_other, gram_rows))

        left, right = pair_half[:, :half], pair_half[:, half:]
        left_t, right_t = pair_other[:, :half].T, pair_other[:, half:].T
        as_first, as_upper = core == 0, side_here == 0

        def put_pair(row, upper):
            first = jnp.where(
                as_first, jnp.where(upper, left, left_t), jnp.where(upper, left_t, right_t)
            )
            second = jnp.where(
                as_first, jnp.where(upper, right, right_t), jnp.where(upper, left, right)
            )
            held_rows = lax.dynamic_update_slice(gram_rows, first, (row, rows))
            return lax.dynamic_update_slice(held_rows, second, (row, rows + half))

        gram_rows = put_pair(0, as_upper)
        gram_rows = put_rung(rung_first, 0, there)
        own_got, gram_rows = lax.optimization_barrier((own_got, gram_rows))
        own.take(own_got)
        own_rows = own.value.reshape(half, rows)
        own_came = swap(own_rows, *over_grp[-1])
        gram_rows = put(own_rows, 0, 0)
        images = [product(gram_rows, whole, half, 0)]
        gram_rows = after(gram_rows, images[0])
        gram_rows = put_rung(rung_own, half, here, there)
        gram_rows = put_pair(half, jnp.logical_not(as_upper))
        gram_rows = put_came(came_first, here)
        gram_rows = put_came(came_second, there)
        gram_rows = put_rung(rung_second, half, there)
        own_came, gram_rows = lax.optimization_barrier((own_came, gram_rows))
        gram_rows = put(own_came, half, 0)
        images.append(product(gram_rows, whole, half, 1))

        def spread(image, *earlier):
            found = [image, on_chip(image)]
            for step in range(1, n_chip):
                got = from_chip(image, step)
                if earlier:
                    got = after(got, *earlier)
                found += [got, on_chip(got)]
            return found

        found_here = spread(images[0], images[1])
        side_there = 1 - side_here
        if half % 128 == 0:
            early = [*found_here, images[1], on_chip(images[1])]
            columns = [2 * slot + side_here for slot in slots]
            columns += [side_there, 2 + side_there, side_here]
            begun = add_terms(
                second_begin_kernel,
                gram_rows,
                jnp.stack(columns),
                early,
                (held, *images),
                jnp.float32,
            )
            late = []
            for step in range(1, n_chip):
                got = after(from_chip(images[1], step), begun)
                late += [got, on_chip(got)]
            columns = [2 * slot + side_there for slot in slots[2:]] + [side_here]
            return add_terms(
                second_end_kernel,
                gram_rows,
                jnp.stack(columns),
                late,
                (begun,),
                jnp.bfloat16,
                scratch=True,
                limit=58 << 20,
            )

        spread_image = in_order(spread(images[1]), there, in_order(found_here, here))
        second_image = jnp.dot(gram_rows, spread_image, preferred_element_type=jnp.float32)
        factor = 0.2 * math.sqrt(COLS)
        update = jnp.zeros(held.shape, jnp.bfloat16)
        for at, start in enumerate((here, there)):
            combined = (
                coef_linear * lax.dynamic_slice_in_dim(held, start, half, 0).astype(jnp.float32)
                + coef_cubic * images[at].astype(jnp.float32)
                + coef_quintic * second_image[at * half : (at + 1) * half]
            )
            update = lax.dynamic_update_slice_in_dim(
                update, (factor * combined).astype(jnp.bfloat16), start, 0
            )
        return update

    return body


def solution(mesh):
    sizes = mesh.shape
    in_specs = (P(("fsdp", "grp", "rep"), None),)
    out_specs = P("fsdp", ("grp", "rep"))
    body = make_body(sizes["fsdp"], sizes["grp"], sizes["rep"])
    return jax.shard_map(body, mesh=mesh, in_specs=in_specs, out_specs=out_specs, check_vma=False)
```

```python
import math

import jax
import jax.numpy as jnp
from jax import lax
from jax.experimental import pallas as pl
from jax.experimental.layout import Layout, with_layout_constraint
from jax.experimental.pallas import tpu as pltpu
from jax.sharding import PartitionSpec as P

COLS = 7168


coef_linear = 3.4445
coef_cubic = -4.775
coef_quintic = 2.0315


def after(value, *earlier):
    return lax.optimization_barrier((value,) + earlier)[0]


def dot_rows(left, right):
    return lax.dot_general(
        left, right, (((1,), (1,)), ((), ())), preferred_element_type=jnp.float32
    ).astype(jnp.bfloat16)


DEPTH = 1024


def accumulate(left, right, total):
    part = jnp.dot(left[...], right[...], preferred_element_type=jnp.float32)

    @pl.when(pl.program_id(0) == 0)
    def _():
        total[...] = part

    @pl.when(pl.program_id(0) > 0)
    def _():
        total[...] += part


def first_kernel(left, right, out, total):
    accumulate(left, right, total)

    @pl.when(pl.program_id(0) == pl.num_programs(0) - 1)
    def _():
        out[...] = total[...].astype(out.dtype)


def product(left, right, rows, row_at):
    depth, width = right.shape
    step = math.gcd(DEPTH, depth)
    return pl.pallas_call(
        first_kernel,
        out_shape=jax.ShapeDtypeStruct((rows, width), jnp.bfloat16),
        grid=(depth // step,),
        in_specs=[
            pl.BlockSpec((rows, step), lambda at: (row_at, at)),
            pl.BlockSpec((step, width), lambda at: (at, 0)),
        ],
        out_specs=pl.BlockSpec((rows, width), lambda at: (0, 0)),
        scratch_shapes=[pltpu.VMEM((rows, width), jnp.float32)],
        compiler_params=pltpu.CompilerParams(vmem_limit_bytes=48 << 20),
    )(left, right)


def second_begin_kernel(count):
    def kernel(columns, left, *refs):
        rights, (held, image_here, image_there, out) = refs[:count], refs[count:]
        factor = 0.2 * math.sqrt(COLS)

        @pl.when(pl.program_id(0) == 0)
        def _():
            half = image_here.shape[0]
            side = columns[count]
            for at, row_half, image in ((0, side, image_here), (half, 1 - side, image_there)):
                held_rows = held[pl.ds(pl.multiple_of(row_half * half, half), half), :]
                out[pl.ds(at, half), :] = factor * (
                    coef_linear * held_rows.astype(jnp.float32)
                    + coef_cubic * image[...].astype(jnp.float32)
                )

        for at, right in enumerate(rights):

            @pl.when(pl.program_id(0) == at)
            def _(right=right):
                part = jnp.dot(left[...], right[...], preferred_element_type=jnp.float32)
                out[...] += (factor * coef_quintic) * part

    return kernel


def second_end_kernel(count):
    def kernel(columns, left, *refs):
        rights, (begun, out, total) = refs[:count], refs[count:]
        factor = 0.2 * math.sqrt(COLS)
        for at, right in enumerate(rights):

            @pl.when(pl.program_id(0) == at)
            def _(at=at, right=right):
                part = jnp.dot(left[...], right[...], preferred_element_type=jnp.float32)
                before = begun if at == 0 else total
                total[...] = before[...] + (factor * coef_quintic) * part

        @pl.when(pl.program_id(0) == count - 1)
        def _():
            half = total.shape[0] // 2
            side = columns[count]
            for at, row_half in ((0, side), (half, 1 - side)):
                rows = pl.ds(pl.multiple_of(row_half * half, half), half)
                out[rows, :] = total[pl.ds(at, half), :].astype(out.dtype)

    return kernel


def add_terms(kernel, gram, columns, rights, others, kind, scratch=False, limit=48 << 20):
    rows = gram.shape[0]
    depth, width = rights[0].shape

    def fixed(value):
        return pl.BlockSpec(
            value.shape, lambda at, columns: (0, 0), pipeline_mode=pl.Buffered(1)
        )

    return pl.pallas_call(
        kernel(len(rights)),
        out_shape=jax.ShapeDtypeStruct((rows, width), kind),
        grid_spec=pltpu.PrefetchScalarGridSpec(
            num_scalar_prefetch=1,
            grid=(len(rights),),
            in_specs=[pl.BlockSpec((rows, depth), lambda at, columns: (0, columns[at]))]
            + [fixed(value) for value in (*rights, *others)],
            out_specs=pl.BlockSpec((rows, width), lambda at, columns: (0, 0)),
            scratch_shapes=[pltpu.VMEM((rows, width), jnp.float32)] if scratch else [],
        ),
        compiler_params=pltpu.CompilerParams(vmem_limit_bytes=limit),
    )(columns, gram, *rights, *others)


def begin_kernel(block, out):
    out[...] = block[...]


def begin_gram(block, columns, column_at):
    rows, width = block.shape
    return pl.pallas_call(
        begin_kernel,
        out_shape=jax.ShapeDtypeStruct((2 * rows, columns * width), block.dtype),
        grid=(1,),
        in_specs=[pl.BlockSpec((rows, width), lambda at: (0, 0))],
        out_specs=pl.BlockSpec((rows, width), lambda at: (0, column_at)),
    )(block)


def by_rows(value):
    return with_layout_constraint(value, Layout(tuple(range(value.ndim))))


def make_body(n_row, n_grp, n_rep):
    n_chip = n_row // 2
    n_col = n_grp * n_rep
    over = ("grp", "rep")
    swap_cores = [(at, at ^ 1) for at in range(n_row)]

    def from_chip(value, step):
        pairs = [(at, (at - 2 * step) % n_row) for at in range(n_row)]
        return lax.ppermute(value, "fsdp", pairs)

    def on_chip(value):
        return lax.ppermute(value, "fsdp", swap_cores)

    def place(at):
        return (at % n_chip) * 2 + (at % n_row) // n_chip

    def ring(value, step):
        pairs = [(place(at), place(at + step)) for at in range(n_row)]
        return lax.ppermute(value, "fsdp", pairs)

    def begin_sum(value):
        assert n_grp & (n_grp - 1) == 0
        bit = 1
        while True:
            rows = value.shape[0] // 2
            side = (lax.axis_index("grp") // bit) % 2
            kept = lax.dynamic_slice_in_dim(value, side * rows, rows, 0)
            sent = lax.dynamic_slice_in_dim(value, (1 - side) * rows, rows, 0)
            got = lax.ppermute(sent, "grp", [(at, at ^ bit) for at in range(n_grp)])
            if 2 * bit == n_grp:
                return kept, sent, got
            value = (kept.astype(jnp.float32) + got.astype(jnp.float32)).astype(value.dtype)
            bit = 2 * bit

    rep_bits = [1 << at for at in range(n_rep.bit_length() - 1)][::-1]
    grp_bits = [1 << at for at in range(n_grp.bit_length() - 1)][::-1]
    over_rep = [("rep", n_rep, bit) for bit in rep_bits]
    over_grp = [("grp", n_grp, bit) for bit in grp_bits]

    def swap(value, axis, size, bit):
        return lax.ppermute(value, axis, [(at, at ^ bit) for at in range(size)])

    def join(value, got, axis, bit, known_grp, known_rep):
        side = (lax.axis_index(axis) // bit) % 2
        lower = jnp.where(side == 0, value, got)
        upper = jnp.where(side == 0, got, value)
        return jnp.stack([lower, upper], axis=0 if axis == "grp" else known_grp + known_rep)

    class Gather:
        def __init__(self, value, steps):
            self.value, self.steps = value, list(steps)
            self.known = {"grp": 0, "rep": 0}

        def send(self):
            return swap(self.value, *self.steps[0])

        def take(self, got):
            axis, _, bit = self.steps.pop(0)
            self.value = join(
                self.value, got, axis, bit, self.known["grp"], self.known["rep"]
            )
            self.known[axis] += 1

    def cut_sum(parts):
        added = [
            (kept.astype(jnp.float32) + got.astype(jnp.float32))
            .astype(kept.dtype)
            .reshape(n_rep, -1, kept.shape[1])
            for kept, got in parts
        ]
        return jnp.concatenate(added, axis=1)

    def to_rep(cut):
        return lax.all_to_all(cut, "rep", split_axis=0, concat_axis=0, tiled=True)

    def end_sum(pieces):
        return jnp.sum(pieces.astype(jnp.float32), axis=0).astype(pieces.dtype)

    def body(iterate):
        at_row = lax.axis_index("fsdp")
        chip, core = at_row // 2, at_row % 2
        held = lax.all_to_all(iterate, over, split_axis=1, concat_axis=0, tiled=True)
        rows, width = held.shape
        half = rows // 2
        cut_at = rows // n_col
        other = on_chip(held)
        far = [from_chip(held, step) for step in range(1, n_chip)]

        slots = [jnp.int32(0), jnp.int32(1)]
        for step in range(1, n_chip):
            near = chip + step < n_chip
            ahead_slot, behind_slot = 2 * step, 2 * (n_chip - step) + 1
            slots.append(jnp.where(near, ahead_slot, behind_slot))
            slots.append(jnp.where(near, behind_slot, ahead_slot))

        def in_order(found, start=0, whole=None):
            size, width = found[0].shape
            if whole is None:
                whole = jnp.zeros((n_row * rows, width), found[0].dtype)
            for at, block in enumerate(found):
                whole = lax.dynamic_update_slice(whole, block, (slots[at] * rows + start, 0))
            return whole

        kept_own, sent_own, got_own = begin_sum(dot_rows(held, held))
        quadrant_at = core * half
        upper = dot_rows(
            after(held[:half], sent_own), lax.dynamic_slice_in_dim(other, quadrant_at, half, 0)
        )
        right = dot_rows(lax.dynamic_slice_in_dim(held, quadrant_at, half, 0), other[half:])
        kept_pair, _, got_pair = begin_sum(jnp.concatenate([upper, right], axis=1))

        panel, started = [held, other], []
        for step in range(1, n_chip):
            far_own, got_own, got_pair = lax.optimization_barrier(
                (far[step - 1], got_own, got_pair)
            )
            far_other = on_chip(far_own)
            panel += [far_own, far_other]
            right = jnp.where(chip + step < n_chip, far_own, far_other)
            started.append(begin_sum(by_rows(dot_rows(held, right))))
        near_pieces = to_rep(cut_sum([(kept_own, got_own), (kept_pair, got_pair)]))
        cut = cut_sum([(kept, got) for kept, _, got in started])
        near_pieces, cut = lax.optimization_barrier((near_pieces, cut))
        near_piece = end_sum(near_pieces)
        own = Gather(near_piece[:cut_at], over_rep + over_grp[:-1])
        pair = Gather(near_piece[cut_at:], over_grp + over_rep)
        while len(pair.steps) > len(over_rep) + 1:
            pair.take(pair.send())
        pair_got = pair.send()
        whole = in_order(panel)
        pieces, pair_got, whole = lax.optimization_barrier((to_rep(cut), pair_got, whole))
        ahead = Gather(end_sum(pieces), over_rep + over_grp[:-1])
        pair.take(pair_got)

        ahead_got = ahead.send()
        ahead.take(ahead_got)
        pair.value = after(pair.value, ahead_got)
        pair_got = pair.send()
        while ahead.steps:
            ahead.take(ahead.send())

        side_here = lax.axis_index("grp") % 2
        here = side_here * half
        there = half - here
        steps = range(1, n_chip)
        own_half = [
            by_rows(ahead.value[..., (at - 1) * cut_at : at * cut_at, :].reshape(half, rows))
            for at in steps
        ]
        def put(block, row, column):
            return lax.dynamic_update_slice(gram_rows, block, (row, column))

        def columns_from(start):
            return [lax.dynamic_slice_in_dim(block, start, half, 1) for block in own_half]

        def ring_all(blocks):
            return [ring(block, at) for at, block in zip(steps, blocks)]

        def swap_all(blocks):
            return [swap(block, *over_grp[-1]) for block in blocks]

        came_first = swap_all(columns_from(there))
        rung_own = ring_all(columns_from(here))
        pair_got, *own_half = lax.optimization_barrier((pair_got, *own_half))
        pair.take(pair_got)
        while len(pair.steps) > 1:
            pair.take(pair.send())
        pair_got = pair.send()
        own.value = after(own.value, *own_half)
        own_got = own.send()
        rung_first = ring_all(came_first)
        later = columns_from(here)
        later[0] = after(later[0], *came_first)
        came_second = swap_all(later)
        later = columns_from(there)
        later[0] = after(later[0], *rung_own)
        rung_other = ring_all(later)
        rung_second = ring_all(came_second)

        gram_rows = begin_gram(own_half[0], n_row, 2)
        for at, block in zip(steps[1:], own_half[1:]):
            gram_rows = put(block, 0, 2 * at * rows)

        def put_came(blocks, column):
            (*blocks, held_rows) = lax.optimization_barrier((*blocks, gram_rows))
            for at, block in zip(steps, blocks):
                held_rows = lax.dynamic_update_slice(
                    held_rows, block, (half, 2 * at * rows + column)
                )
            return held_rows

        def put_rung(blocks, row, column):
            (*blocks, held_rows) = lax.optimization_barrier((*blocks, gram_rows))
            for at, block in zip(steps, blocks):
                held_rows = lax.dynamic_update_slice(
                    held_rows, block.T, (row, (2 * at + 1) * rows + column)
                )
            return held_rows

        pair_got, own_got, gram_rows, *_ = lax.optimization_barrier(
            (pair_got, own_got, gram_rows, *came_first, *rung_own)
        )
        pair.take(pair_got)
        pair_half = pair.value.reshape(half, rows)
        pair_other = on_chip(pair_half)
        own.take(own_got)
        while len(own.steps) > 1:
            own.take(own.send())
        own_got = own.send()
        gram_rows = after(gram_rows, own.value)
        gram_rows = put_rung(rung_own, 0, here)
        pair_other, gram_rows = lax.optimization_barrier((pair_other, gram_rows))

        left, right = pair_half[:, :half], pair_half[:, half:]
        left_t, right_t = pair_other[:, :half].T, pair_other[:, half:].T
        as_first, as_upper = core == 0, side_here == 0

        def put_pair(row, upper):
            first = jnp.where(
                as_first, jnp.where(upper, left, left_t), jnp.where(upper, left_t, right_t)
            )
            second = jnp.where(
                as_first, jnp.where(upper, right, right_t), jnp.where(upper, left, right)
            )
            held_rows = lax.dynamic_update_slice(gram_rows, first, (row, rows))
            return lax.dynamic_update_slice(held_rows, second, (row, rows + half))

        gram_rows = put_pair(0, as_upper)
        gram_rows = after(gram_rows, *came_second)
        gram_rows = put_rung(rung_first, 0, there)
        own_got, gram_rows = lax.optimization_barrier((own_got, gram_rows))
        own.take(own_got)
        own_rows = own.value.reshape(half, rows)
        own_came = swap(own_rows, *over_grp[-1])
        gram_rows = put(own_rows, 0, 0)
        images = [product(gram_rows, whole, half, 0)]
        gram_rows = after(gram_rows, images[0])
        gram_rows = put_rung(rung_other, half, here)
        gram_rows = put_pair(half, jnp.logical_not(as_upper))
        gram_rows = put_came(came_first, here)
        gram_rows = put_came(came_second, there)
        gram_rows = put_rung(rung_second, half, there)
        own_came, gram_rows = lax.optimization_barrier((own_came, gram_rows))
        gram_rows = put(own_came, half, 0)
        images.append(product(gram_rows, whole, half, 1))

        def spread(image, *earlier):
            found = [image, on_chip(image)]
            for step in range(1, n_chip):
                got = from_chip(image, step)
                if earlier:
                    got = after(got, *earlier)
                found += [got, on_chip(got)]
            return found

        found_here = spread(images[0], images[1])
        side_there = 1 - side_here
        if half % 128 == 0:
            early = [*found_here, images[1], on_chip(images[1])]
            columns = [2 * slot + side_here for slot in slots]
            columns += [side_there, 2 + side_there, side_here]
            begun = add_terms(
                second_begin_kernel,
                gram_rows,
                jnp.stack(columns),
                early,
                (held, *images),
                jnp.float32,
            )
            late = []
            for step in range(1, n_chip):
                got = after(from_chip(images[1], step), begun)
                late += [got, on_chip(got)]
            columns = [2 * slot + side_there for slot in slots[2:]] + [side_here]
            return add_terms(
                second_end_kernel,
                gram_rows,
                jnp.stack(columns),
                late,
                (begun,),
                jnp.bfloat16,
                scratch=True,
                limit=58 << 20,
            )

        spread_image = in_order(spread(images[1]), there, in_order(found_here, here))
        second_image = jnp.dot(gram_rows, spread_image, preferred_element_type=jnp.float32)
        factor = 0.2 * math.sqrt(COLS)
        update = jnp.zeros(held.shape, jnp.bfloat16)
        for at, start in enumerate((here, there)):
            combined = (
                coef_linear * lax.dynamic_slice_in_dim(held, start, half, 0).astype(jnp.float32)
                + coef_cubic * images[at].astype(jnp.float32)
                + coef_quintic * second_image[at * half : (at + 1) * half]
            )
            update = lax.dynamic_update_slice_in_dim(
                update, (factor * combined).astype(jnp.bfloat16), start, 0
            )
        return update

    return body


def solution(mesh):
    sizes = mesh.shape
    in_specs = (P(("fsdp", "grp", "rep"), None),)
    out_specs = P("fsdp", ("grp", "rep"))
    body = make_body(sizes["fsdp"], sizes["grp"], sizes["rep"])
    return jax.shard_map(body, mesh=mesh, in_specs=in_specs, out_specs=out_specs, check_vma=False)
```

```python
import math

import jax
import jax.numpy as jnp
from jax import lax
from jax.experimental import pallas as pl
from jax.experimental.layout import Layout, with_layout_constraint
from jax.experimental.pallas import tpu as pltpu
from jax.sharding import PartitionSpec as P

COLS = 7168


coef_linear = 3.4445
coef_cubic = -4.775
coef_quintic = 2.0315


def after(value, *earlier):
    return lax.optimization_barrier((value,) + earlier)[0]


def dot_rows(left, right):
    return lax.dot_general(
        left, right, (((1,), (1,)), ((), ())), preferred_element_type=jnp.float32
    ).astype(jnp.bfloat16)


DEPTH = 1024


def accumulate(left, right, total):
    part = jnp.dot(left[...], right[...], preferred_element_type=jnp.float32)

    @pl.when(pl.program_id(0) == 0)
    def _():
        total[...] = part

    @pl.when(pl.program_id(0) > 0)
    def _():
        total[...] += part


def first_kernel(left, right, out, total):
    accumulate(left, right, total)

    @pl.when(pl.program_id(0) == pl.num_programs(0) - 1)
    def _():
        out[...] = total[...].astype(out.dtype)


def product(left, right, rows, row_at):
    depth, width = right.shape
    step = math.gcd(DEPTH, depth)
    return pl.pallas_call(
        first_kernel,
        out_shape=jax.ShapeDtypeStruct((rows, width), jnp.bfloat16),
        grid=(depth // step,),
        in_specs=[
            pl.BlockSpec((rows, step), lambda at: (row_at, at)),
            pl.BlockSpec((step, width), lambda at: (at, 0)),
        ],
        out_specs=pl.BlockSpec((rows, width), lambda at: (0, 0)),
        scratch_shapes=[pltpu.VMEM((rows, width), jnp.float32)],
        compiler_params=pltpu.CompilerParams(vmem_limit_bytes=48 << 20),
    )(left, right)


def second_begin_kernel(count):
    def kernel(columns, left, *refs):
        rights, (held, image_here, image_there, out) = refs[:count], refs[count:]
        factor = 0.2 * math.sqrt(COLS)

        @pl.when(pl.program_id(0) == 0)
        def _():
            half = image_here.shape[0]
            side = columns[count]
            for at, row_half, image in ((0, side, image_here), (half, 1 - side, image_there)):
                held_rows = held[pl.ds(pl.multiple_of(row_half * half, half), half), :]
                out[pl.ds(at, half), :] = factor * (
                    coef_linear * held_rows.astype(jnp.float32)
                    + coef_cubic * image[...].astype(jnp.float32)
                )

        for at, right in enumerate(rights):

            @pl.when(pl.program_id(0) == at)
            def _(right=right):
                part = jnp.dot(left[...], right[...], preferred_element_type=jnp.float32)
                out[...] += (factor * coef_quintic) * part

    return kernel


def second_end_kernel(count):
    def kernel(columns, left, *refs):
        rights, (begun, out, total) = refs[:count], refs[count:]
        factor = 0.2 * math.sqrt(COLS)
        for at, right in enumerate(rights):

            @pl.when(pl.program_id(0) == at)
            def _(at=at, right=right):
                part = jnp.dot(left[...], right[...], preferred_element_type=jnp.float32)
                before = begun if at == 0 else total
                total[...] = before[...] + (factor * coef_quintic) * part

        @pl.when(pl.program_id(0) == count - 1)
        def _():
            half = total.shape[0] // 2
            side = columns[count]
            for at, row_half in ((0, side), (half, 1 - side)):
                rows = pl.ds(pl.multiple_of(row_half * half, half), half)
                out[rows, :] = total[pl.ds(at, half), :].astype(out.dtype)

    return kernel


def add_terms(kernel, gram, columns, rights, others, kind, scratch=False, limit=48 << 20):
    rows = gram.shape[0]
    depth, width = rights[0].shape

    def fixed(value):
        return pl.BlockSpec(
            value.shape, lambda at, columns: (0, 0), pipeline_mode=pl.Buffered(1)
        )

    return pl.pallas_call(
        kernel(len(rights)),
        out_shape=jax.ShapeDtypeStruct((rows, width), kind),
        grid_spec=pltpu.PrefetchScalarGridSpec(
            num_scalar_prefetch=1,
            grid=(len(rights),),
            in_specs=[pl.BlockSpec((rows, depth), lambda at, columns: (0, columns[at]))]
            + [fixed(value) for value in (*rights, *others)],
            out_specs=pl.BlockSpec((rows, width), lambda at, columns: (0, 0)),
            scratch_shapes=[pltpu.VMEM((rows, width), jnp.float32)] if scratch else [],
        ),
        compiler_params=pltpu.CompilerParams(vmem_limit_bytes=limit),
    )(columns, gram, *rights, *others)


def begin_kernel(block, out):
    out[...] = block[...]


def begin_gram(block, columns, column_at):
    rows, width = block.shape
    return pl.pallas_call(
        begin_kernel,
        out_shape=jax.ShapeDtypeStruct((2 * rows, columns * width), block.dtype),
        grid=(1,),
        in_specs=[pl.BlockSpec((rows, width), lambda at: (0, 0))],
        out_specs=pl.BlockSpec((rows, width), lambda at: (0, column_at)),
    )(block)


def by_rows(value):
    return with_layout_constraint(value, Layout(tuple(range(value.ndim))))


def make_body(n_row, n_grp, n_rep):
    n_chip = n_row // 2
    n_col = n_grp * n_rep
    over = ("grp", "rep")
    swap_cores = [(at, at ^ 1) for at in range(n_row)]

    def from_chip(value, step):
        pairs = [(at, (at - 2 * step) % n_row) for at in range(n_row)]
        return lax.ppermute(value, "fsdp", pairs)

    def on_chip(value):
        return lax.ppermute(value, "fsdp", swap_cores)

    def place(at):
        return (at % n_chip) * 2 + (at % n_row) // n_chip

    def ring(value, step):
        pairs = [(place(at), place(at + step)) for at in range(n_row)]
        return lax.ppermute(value, "fsdp", pairs)

    def begin_sum(value):
        assert n_grp & (n_grp - 1) == 0
        bit = 1
        while True:
            rows = value.shape[0] // 2
            side = (lax.axis_index("grp") // bit) % 2
            kept = lax.dynamic_slice_in_dim(value, side * rows, rows, 0)
            sent = lax.dynamic_slice_in_dim(value, (1 - side) * rows, rows, 0)
            got = lax.ppermute(sent, "grp", [(at, at ^ bit) for at in range(n_grp)])
            if 2 * bit == n_grp:
                return kept, sent, got
            value = (kept.astype(jnp.float32) + got.astype(jnp.float32)).astype(value.dtype)
            bit = 2 * bit

    rep_bits = [1 << at for at in range(n_rep.bit_length() - 1)][::-1]
    grp_bits = [1 << at for at in range(n_grp.bit_length() - 1)][::-1]
    over_rep = [("rep", n_rep, bit) for bit in rep_bits]
    over_grp = [("grp", n_grp, bit) for bit in grp_bits]

    def swap(value, axis, size, bit):
        return lax.ppermute(value, axis, [(at, at ^ bit) for at in range(size)])

    def join(value, got, axis, bit, known_grp, known_rep):
        side = (lax.axis_index(axis) // bit) % 2
        lower = jnp.where(side == 0, value, got)
        upper = jnp.where(side == 0, got, value)
        return jnp.stack([lower, upper], axis=0 if axis == "grp" else known_grp + known_rep)

    class Gather:
        def __init__(self, value, steps):
            self.value, self.steps = value, list(steps)
            self.known = {"grp": 0, "rep": 0}

        def send(self):
            return swap(self.value, *self.steps[0])

        def take(self, got):
            axis, _, bit = self.steps.pop(0)
            self.value = join(
                self.value, got, axis, bit, self.known["grp"], self.known["rep"]
            )
            self.known[axis] += 1

    def cut_sum(parts):
        added = [
            (kept.astype(jnp.float32) + got.astype(jnp.float32))
            .astype(kept.dtype)
            .reshape(n_rep, -1, kept.shape[1])
            for kept, got in parts
        ]
        return jnp.concatenate(added, axis=1)

    def to_rep(cut):
        return lax.all_to_all(cut, "rep", split_axis=0, concat_axis=0, tiled=True)

    def end_sum(pieces):
        return jnp.sum(pieces.astype(jnp.float32), axis=0).astype(pieces.dtype)

    def body(iterate):
        at_row = lax.axis_index("fsdp")
        chip, core = at_row // 2, at_row % 2
        held = lax.all_to_all(iterate, over, split_axis=1, concat_axis=0, tiled=True)
        rows, width = held.shape
        half = rows // 2
        cut_at = rows // n_col
        other = on_chip(held)
        far = [from_chip(held, step) for step in range(1, n_chip)]

        slots = [jnp.int32(0), jnp.int32(1)]
        for step in range(1, n_chip):
            near = chip + step < n_chip
            ahead_slot, behind_slot = 2 * step, 2 * (n_chip - step) + 1
            slots.append(jnp.where(near, ahead_slot, behind_slot))
            slots.append(jnp.where(near, behind_slot, ahead_slot))

        def in_order(found, start=0, whole=None):
            size, width = found[0].shape
            if whole is None:
                whole = jnp.zeros((n_row * rows, width), found[0].dtype)
            for at, block in enumerate(found):
                whole = lax.dynamic_update_slice(whole, block, (slots[at] * rows + start, 0))
            return whole

        kept_own, sent_own, got_own = begin_sum(dot_rows(held, held))
        quadrant_at = core * half
        upper = dot_rows(
            after(held[:half], sent_own), lax.dynamic_slice_in_dim(other, quadrant_at, half, 0)
        )
        right = dot_rows(lax.dynamic_slice_in_dim(held, quadrant_at, half, 0), other[half:])
        kept_pair, _, got_pair = begin_sum(jnp.concatenate([upper, right], axis=1))

        panel, started = [held, other], []
        for step in range(1, n_chip):
            far_own, got_own, got_pair = lax.optimization_barrier(
                (far[step - 1], got_own, got_pair)
            )
            far_other = on_chip(far_own)
            panel += [far_own, far_other]
            right = jnp.where(chip + step < n_chip, far_own, far_other)
            started.append(begin_sum(by_rows(dot_rows(held, right))))
        near_pieces = to_rep(cut_sum([(kept_own, got_own), (kept_pair, got_pair)]))
        cut = cut_sum([(kept, got) for kept, _, got in started])
        near_pieces, cut = lax.optimization_barrier((near_pieces, cut))
        near_piece = end_sum(near_pieces)
        own = Gather(near_piece[:cut_at], over_rep + over_grp[:-1])
        pair = Gather(near_piece[cut_at:], over_grp + over_rep)
        while len(pair.steps) > len(over_rep) + 1:
            pair.take(pair.send())
        pair_got = pair.send()
        whole = in_order(panel)
        pieces, pair_got, whole = lax.optimization_barrier((to_rep(cut), pair_got, whole))
        ahead = Gather(end_sum(pieces), over_rep + over_grp[:-1])
        pair.take(pair_got)

        ahead_got = ahead.send()
        ahead.take(ahead_got)
        pair.value = after(pair.value, ahead_got)
        pair_got = pair.send()
        while ahead.steps:
            ahead.take(ahead.send())

        side_here = lax.axis_index("grp") % 2
        here = side_here * half
        there = half - here
        steps = range(1, n_chip)
        own_half = [
            by_rows(ahead.value[..., (at - 1) * cut_at : at * cut_at, :].reshape(half, rows))
            for at in steps
        ]
        def put(block, row, column):
            return lax.dynamic_update_slice(gram_rows, block, (row, column))

        def columns_from(start):
            return [lax.dynamic_slice_in_dim(block, start, half, 1) for block in own_half]

        def ring_all(blocks):
            return [ring(block, at) for at, block in zip(steps, blocks)]

        def swap_all(blocks):
            return [swap(block, *over_grp[-1]) for block in blocks]

        came_first = swap_all(columns_from(there))
        rung_own = ring_all(columns_from(here))
        pair_got, *own_half = lax.optimization_barrier((pair_got, *own_half))
        pair.take(pair_got)
        while len(pair.steps) > 1:
            pair.take(pair.send())
        pair_got = pair.send()
        own.value = after(own.value, *own_half)
        own_got = own.send()
        rung_first = ring_all(came_first)
        later = columns_from(here)
        later[0] = after(later[0], *came_first)
        came_second = swap_all(later)
        later = columns_from(there)
        later[0] = after(later[0], *rung_own)
        rung_other = ring_all(later)
        rung_second = ring_all(came_second)

        gram_rows = begin_gram(own_half[0], n_row, 2)
        for at, block in zip(steps[1:], own_half[1:]):
            gram_rows = put(block, 0, 2 * at * rows)

        def put_came(blocks, column):
            (*blocks, held_rows) = lax.optimization_barrier((*blocks, gram_rows))
            for at, block in zip(steps, blocks):
                held_rows = lax.dynamic_update_slice(
                    held_rows, block, (half, 2 * at * rows + column)
                )
            return held_rows

        def put_rung(blocks, row, column):
            (*blocks, held_rows) = lax.optimization_barrier((*blocks, gram_rows))
            for at, block in zip(steps, blocks):
                held_rows = lax.dynamic_update_slice(
                    held_rows, block.T, (row, (2 * at + 1) * rows + column)
                )
            return held_rows

        pair_got, own_got, gram_rows, *_ = lax.optimization_barrier(
            (pair_got, own_got, gram_rows, *came_first)
        )
        pair.take(pair_got)
        pair_half = pair.value.reshape(half, rows)
        pair_other = on_chip(pair_half)
        own.take(own_got)
        while len(own.steps) > 1:
            own.take(own.send())
        own_got = own.send()
        gram_rows = put_rung(rung_own, 0, here)
        gram_rows = after(gram_rows, own.value, *came_second)
        gram_rows = put_rung(rung_first, 0, there)
        pair_other, gram_rows = lax.optimization_barrier((pair_other, gram_rows))

        left, right = pair_half[:, :half], pair_half[:, half:]
        left_t, right_t = pair_other[:, :half].T, pair_other[:, half:].T
        as_first, as_upper = core == 0, side_here == 0

        def put_pair(row, upper):
            first = jnp.where(
                as_first, jnp.where(upper, left, left_t), jnp.where(upper, left_t, right_t)
            )
            second = jnp.where(
                as_first, jnp.where(upper, right, right_t), jnp.where(upper, left, right)
            )
            held_rows = lax.dynamic_update_slice(gram_rows, first, (row, rows))
            return lax.dynamic_update_slice(held_rows, second, (row, rows + half))

        gram_rows = put_pair(0, as_upper)
        own_got, gram_rows = lax.optimization_barrier((own_got, gram_rows))
        own.take(own_got)
        own_rows = own.value.reshape(half, rows)
        own_came = swap(own_rows, *over_grp[-1])
        gram_rows = put(own_rows, 0, 0)
        images = [product(gram_rows, whole, half, 0)]
        gram_rows = after(gram_rows, images[0])
        gram_rows = put_rung(rung_other, half, here)
        gram_rows = put_pair(half, jnp.logical_not(as_upper))
        gram_rows = put_came(came_first, here)
        gram_rows = put_came(came_second, there)
        gram_rows = put_rung(rung_second, half, there)
        own_came, gram_rows = lax.optimization_barrier((own_came, gram_rows))
        gram_rows = put(own_came, half, 0)
        images.append(product(gram_rows, whole, half, 1))

        def spread(image, *earlier):
            found = [image, on_chip(image)]
            for step in range(1, n_chip):
                got = from_chip(image, step)
                if earlier:
                    got = after(got, *earlier)
                found += [got, on_chip(got)]
            return found

        found_here = spread(images[0], images[1])
        side_there = 1 - side_here
        if half % 128 == 0:
            early = [*found_here, images[1], on_chip(images[1])]
            columns = [2 * slot + side_here for slot in slots]
            columns += [side_there, 2 + side_there, side_here]
            begun = add_terms(
                second_begin_kernel,
                gram_rows,
                jnp.stack(columns),
                early,
                (held, *images),
                jnp.float32,
            )
            late = []
            for step in range(1, n_chip):
                got = after(from_chip(images[1], step), begun)
                late += [got, on_chip(got)]
            columns = [2 * slot + side_there for slot in slots[2:]] + [side_here]
            return add_terms(
                second_end_kernel,
                gram_rows,
                jnp.stack(columns),
                late,
                (begun,),
                jnp.bfloat16,
                scratch=True,
                limit=58 << 20,
            )

        spread_image = in_order(spread(images[1]), there, in_order(found_here, here))
        second_image = jnp.dot(gram_rows, spread_image, preferred_element_type=jnp.float32)
        factor = 0.2 * math.sqrt(COLS)
        update = jnp.zeros(held.shape, jnp.bfloat16)
        for at, start in enumerate((here, there)):
            combined = (
                coef_linear * lax.dynamic_slice_in_dim(held, start, half, 0).astype(jnp.float32)
                + coef_cubic * images[at].astype(jnp.float32)
                + coef_quintic * second_image[at * half : (at + 1) * half]
            )
            update = lax.dynamic_update_slice_in_dim(
                update, (factor * combined).astype(jnp.bfloat16), start, 0
            )
        return update

    return body


def solution(mesh):
    sizes = mesh.shape
    in_specs = (P(("fsdp", "grp", "rep"), None),)
    out_specs = P("fsdp", ("grp", "rep"))
    body = make_body(sizes["fsdp"], sizes["grp"], sizes["rep"])
    return jax.shard_map(body, mesh=mesh, in_specs=in_specs, out_specs=out_specs, check_vma=False)
```

```python
import math

import jax
import jax.numpy as jnp
from jax import lax
from jax.experimental import pallas as pl
from jax.experimental.layout import Layout, with_layout_constraint
from jax.experimental.pallas import tpu as pltpu
from jax.sharding import PartitionSpec as P

COLS = 7168


coef_linear = 3.4445
coef_cubic = -4.775
coef_quintic = 2.0315


def after(value, *earlier):
    return lax.optimization_barrier((value,) + earlier)[0]


def dot_rows(left, right):
    return lax.dot_general(
        left, right, (((1,), (1,)), ((), ())), preferred_element_type=jnp.float32
    ).astype(jnp.bfloat16)


DEPTH = 1024


def accumulate(left, right, total):
    part = jnp.dot(left[...], right[...], preferred_element_type=jnp.float32)

    @pl.when(pl.program_id(0) == 0)
    def _():
        total[...] = part

    @pl.when(pl.program_id(0) > 0)
    def _():
        total[...] += part


def first_kernel(left, right, out, total):
    accumulate(left, right, total)

    @pl.when(pl.program_id(0) == pl.num_programs(0) - 1)
    def _():
        out[...] = total[...].astype(out.dtype)


def product(left, right, rows, row_at):
    depth, width = right.shape
    step = math.gcd(DEPTH, depth)
    return pl.pallas_call(
        first_kernel,
        out_shape=jax.ShapeDtypeStruct((rows, width), jnp.bfloat16),
        grid=(depth // step,),
        in_specs=[
            pl.BlockSpec((rows, step), lambda at: (row_at, at)),
            pl.BlockSpec((step, width), lambda at: (at, 0)),
        ],
        out_specs=pl.BlockSpec((rows, width), lambda at: (0, 0)),
        scratch_shapes=[pltpu.VMEM((rows, width), jnp.float32)],
        compiler_params=pltpu.CompilerParams(vmem_limit_bytes=48 << 20),
    )(left, right)


def second_begin_kernel(count):
    def kernel(columns, left, *refs):
        rights, (held, image_here, image_there, out) = refs[:count], refs[count:]
        factor = 0.2 * math.sqrt(COLS)

        @pl.when(pl.program_id(0) == 0)
        def _():
            half = image_here.shape[0]
            side = columns[count]
            for at, row_half, image in ((0, side, image_here), (half, 1 - side, image_there)):
                held_rows = held[pl.ds(pl.multiple_of(row_half * half, half), half), :]
                out[pl.ds(at, half), :] = factor * (
                    coef_linear * held_rows.astype(jnp.float32)
                    + coef_cubic * image[...].astype(jnp.float32)
                )

        for at, right in enumerate(rights):

            @pl.when(pl.program_id(0) == at)
            def _(right=right):
                part = jnp.dot(left[...], right[...], preferred_element_type=jnp.float32)
                out[...] += (factor * coef_quintic) * part

    return kernel


def second_end_kernel(count):
    def kernel(columns, left, *refs):
        rights, (begun, out, total) = refs[:count], refs[count:]
        factor = 0.2 * math.sqrt(COLS)
        for at, right in enumerate(rights):

            @pl.when(pl.program_id(0) == at)
            def _(at=at, right=right):
                part = jnp.dot(left[...], right[...], preferred_element_type=jnp.float32)
                before = begun if at == 0 else total
                total[...] = before[...] + (factor * coef_quintic) * part

        @pl.when(pl.program_id(0) == count - 1)
        def _():
            half = total.shape[0] // 2
            side = columns[count]
            for at, row_half in ((0, side), (half, 1 - side)):
                rows = pl.ds(pl.multiple_of(row_half * half, half), half)
                out[rows, :] = total[pl.ds(at, half), :].astype(out.dtype)

    return kernel


def add_terms(kernel, gram, columns, rights, others, kind, scratch=False, limit=48 << 20):
    rows = gram.shape[0]
    depth, width = rights[0].shape

    def fixed(value):
        return pl.BlockSpec(
            value.shape, lambda at, columns: (0, 0), pipeline_mode=pl.Buffered(1)
        )

    return pl.pallas_call(
        kernel(len(rights)),
        out_shape=jax.ShapeDtypeStruct((rows, width), kind),
        grid_spec=pltpu.PrefetchScalarGridSpec(
            num_scalar_prefetch=1,
            grid=(len(rights),),
            in_specs=[pl.BlockSpec((rows, depth), lambda at, columns: (0, columns[at]))]
            + [fixed(value) for value in (*rights, *others)],
            out_specs=pl.BlockSpec((rows, width), lambda at, columns: (0, 0)),
            scratch_shapes=[pltpu.VMEM((rows, width), jnp.float32)] if scratch else [],
        ),
        compiler_params=pltpu.CompilerParams(vmem_limit_bytes=limit),
    )(columns, gram, *rights, *others)


def begin_kernel(block, out):
    out[...] = block[...]


def begin_gram(block, columns, column_at):
    rows, width = block.shape
    return pl.pallas_call(
        begin_kernel,
        out_shape=jax.ShapeDtypeStruct((2 * rows, columns * width), block.dtype),
        grid=(1,),
        in_specs=[pl.BlockSpec((rows, width), lambda at: (0, 0))],
        out_specs=pl.BlockSpec((rows, width), lambda at: (0, column_at)),
    )(block)


def by_rows(value):
    return with_layout_constraint(value, Layout(tuple(range(value.ndim))))


def make_body(n_row, n_grp, n_rep):
    n_chip = n_row // 2
    n_col = n_grp * n_rep
    over = ("grp", "rep")
    swap_cores = [(at, at ^ 1) for at in range(n_row)]

    def from_chip(value, step):
        pairs = [(at, (at - 2 * step) % n_row) for at in range(n_row)]
        return lax.ppermute(value, "fsdp", pairs)

    def on_chip(value):
        return lax.ppermute(value, "fsdp", swap_cores)

    def place(at):
        return (at % n_chip) * 2 + (at % n_row) // n_chip

    def ring(value, step):
        pairs = [(place(at), place(at + step)) for at in range(n_row)]
        return lax.ppermute(value, "fsdp", pairs)

    def begin_sum(value):
        assert n_grp & (n_grp - 1) == 0
        bit = 1
        while True:
            rows = value.shape[0] // 2
            side = (lax.axis_index("grp") // bit) % 2
            kept = lax.dynamic_slice_in_dim(value, side * rows, rows, 0)
            sent = lax.dynamic_slice_in_dim(value, (1 - side) * rows, rows, 0)
            got = lax.ppermute(sent, "grp", [(at, at ^ bit) for at in range(n_grp)])
            if 2 * bit == n_grp:
                return kept, sent, got
            value = (kept.astype(jnp.float32) + got.astype(jnp.float32)).astype(value.dtype)
            bit = 2 * bit

    rep_bits = [1 << at for at in range(n_rep.bit_length() - 1)][::-1]
    grp_bits = [1 << at for at in range(n_grp.bit_length() - 1)][::-1]
    over_rep = [("rep", n_rep, bit) for bit in rep_bits]
    over_grp = [("grp", n_grp, bit) for bit in grp_bits]

    def swap(value, axis, size, bit):
        return lax.ppermute(value, axis, [(at, at ^ bit) for at in range(size)])

    def join(value, got, axis, bit, known_grp, known_rep):
        side = (lax.axis_index(axis) // bit) % 2
        lower = jnp.where(side == 0, value, got)
        upper = jnp.where(side == 0, got, value)
        return jnp.stack([lower, upper], axis=0 if axis == "grp" else known_grp + known_rep)

    class Gather:
        def __init__(self, value, steps):
            self.value, self.steps = value, list(steps)
            self.known = {"grp": 0, "rep": 0}

        def send(self):
            return swap(self.value, *self.steps[0])

        def take(self, got):
            axis, _, bit = self.steps.pop(0)
            self.value = join(
                self.value, got, axis, bit, self.known["grp"], self.known["rep"]
            )
            self.known[axis] += 1

    def cut_sum(parts):
        added = [
            (kept.astype(jnp.float32) + got.astype(jnp.float32))
            .astype(kept.dtype)
            .reshape(n_rep, -1, kept.shape[1])
            for kept, got in parts
        ]
        return jnp.concatenate(added, axis=1)

    def to_rep(cut):
        return lax.all_to_all(cut, "rep", split_axis=0, concat_axis=0, tiled=True)

    def end_sum(pieces):
        return jnp.sum(pieces.astype(jnp.float32), axis=0).astype(pieces.dtype)

    def body(iterate):
        at_row = lax.axis_index("fsdp")
        chip, core = at_row // 2, at_row % 2
        held = lax.all_to_all(iterate, over, split_axis=1, concat_axis=0, tiled=True)
        rows, width = held.shape
        half = rows // 2
        cut_at = rows // n_col
        other = on_chip(held)
        far = [from_chip(held, step) for step in range(1, n_chip)]

        slots = [jnp.int32(0), jnp.int32(1)]
        for step in range(1, n_chip):
            near = chip + step < n_chip
            ahead_slot, behind_slot = 2 * step, 2 * (n_chip - step) + 1
            slots.append(jnp.where(near, ahead_slot, behind_slot))
            slots.append(jnp.where(near, behind_slot, ahead_slot))

        def in_order(found, start=0, whole=None):
            size, width = found[0].shape
            if whole is None:
                whole = jnp.zeros((n_row * rows, width), found[0].dtype)
            for at, block in enumerate(found):
                whole = lax.dynamic_update_slice(whole, block, (slots[at] * rows + start, 0))
            return whole

        kept_own, sent_own, got_own = begin_sum(dot_rows(held, held))
        quadrant_at = core * half
        upper = dot_rows(
            after(held[:half], sent_own), lax.dynamic_slice_in_dim(other, quadrant_at, half, 0)
        )
        right = dot_rows(lax.dynamic_slice_in_dim(held, quadrant_at, half, 0), other[half:])
        kept_pair, _, got_pair = begin_sum(jnp.concatenate([upper, right], axis=1))

        panel, started = [held, other], []
        for step in range(1, n_chip):
            far_own, got_own, got_pair = lax.optimization_barrier(
                (far[step - 1], got_own, got_pair)
            )
            far_other = on_chip(far_own)
            panel += [far_own, far_other]
            right = jnp.where(chip + step < n_chip, far_own, far_other)
            started.append(begin_sum(by_rows(dot_rows(held, right))))
        near_pieces = to_rep(cut_sum([(kept_own, got_own), (kept_pair, got_pair)]))
        cut = cut_sum([(kept, got) for kept, _, got in started])
        near_pieces, cut = lax.optimization_barrier((near_pieces, cut))
        near_piece = end_sum(near_pieces)
        own = Gather(near_piece[:cut_at], over_rep + over_grp[:-1])
        pair = Gather(near_piece[cut_at:], over_grp + over_rep)
        while len(pair.steps) > len(over_rep) + 1:
            pair.take(pair.send())
        pair_got = pair.send()
        whole = in_order(panel)
        pieces, pair_got, whole = lax.optimization_barrier((to_rep(cut), pair_got, whole))
        ahead = Gather(end_sum(pieces), over_rep + over_grp[:-1])
        pair.take(pair_got)

        ahead_got = ahead.send()
        ahead.take(ahead_got)
        pair.value = after(pair.value, ahead_got)
        pair_got = pair.send()
        while ahead.steps:
            ahead.take(ahead.send())

        side_here = lax.axis_index("grp") % 2
        here = side_here * half
        there = half - here
        steps = range(1, n_chip)
        own_half = [
            by_rows(ahead.value[..., (at - 1) * cut_at : at * cut_at, :].reshape(half, rows))
            for at in steps
        ]
        def put(block, row, column):
            return lax.dynamic_update_slice(gram_rows, block, (row, column))

        def columns_from(start):
            return [lax.dynamic_slice_in_dim(block, start, half, 1) for block in own_half]

        def ring_all(blocks):
            return [ring(block, at) for at, block in zip(steps, blocks)]

        def swap_all(blocks):
            return [swap(block, *over_grp[-1]) for block in blocks]

        came_first = swap_all(columns_from(there))
        rung_own = ring_all(columns_from(here))
        pair_got, *own_half = lax.optimization_barrier((pair_got, *own_half))
        pair.take(pair_got)
        while len(pair.steps) > 1:
            pair.take(pair.send())
        pair_got = pair.send()
        own.value = after(own.value, *own_half)
        own_got = own.send()
        rung_first = ring_all(came_first)
        later = columns_from(here)
        later[0] = after(later[0], *came_first)
        came_second = swap_all(later)
        later = columns_from(there)
        later[0] = after(later[0], *rung_own)
        rung_other = ring_all(later)
        rung_second = ring_all(came_second)

        gram_rows = begin_gram(own_half[0], n_row, 2)
        for at, block in zip(steps[1:], own_half[1:]):
            gram_rows = put(block, 0, 2 * at * rows)

        def put_came(blocks, column):
            (*blocks, held_rows) = lax.optimization_barrier((*blocks, gram_rows))
            for at, block in zip(steps, blocks):
                held_rows = lax.dynamic_update_slice(
                    held_rows, block, (half, 2 * at * rows + column)
                )
            return held_rows

        def put_rung(blocks, row, column):
            (*blocks, held_rows) = lax.optimization_barrier((*blocks, gram_rows))
            for at, block in zip(steps, blocks):
                held_rows = lax.dynamic_update_slice(
                    held_rows, block.T, (row, (2 * at + 1) * rows + column)
                )
            return held_rows

        pair_got, own_got, gram_rows, *_ = lax.optimization_barrier(
            (pair_got, own_got, gram_rows, *came_first)
        )
        pair.take(pair_got)
        pair_half = pair.value.reshape(half, rows)
        pair_other = on_chip(pair_half)
        own.take(own_got)
        while len(own.steps) > 1:
            own.take(own.send())
        own_got = own.send()
        gram_rows = put_rung(rung_own, 0, here)
        gram_rows = after(gram_rows, own.value)
        pair_other, gram_rows = lax.optimization_barrier((pair_other, gram_rows))

        left, right = pair_half[:, :half], pair_half[:, half:]
        left_t, right_t = pair_other[:, :half].T, pair_other[:, half:].T
        as_first, as_upper = core == 0, side_here == 0

        def put_pair(row, upper):
            first = jnp.where(
                as_first, jnp.where(upper, left, left_t), jnp.where(upper, left_t, right_t)
            )
            second = jnp.where(
                as_first, jnp.where(upper, right, right_t), jnp.where(upper, left, right)
            )
            held_rows = lax.dynamic_update_slice(gram_rows, first, (row, rows))
            return lax.dynamic_update_slice(held_rows, second, (row, rows + half))

        gram_rows = put_pair(0, as_upper)
        gram_rows = after(gram_rows, *came_second)
        gram_rows = put_rung(rung_first, 0, there)
        own_got, gram_rows = lax.optimization_barrier((own_got, gram_rows))
        own.take(own_got)
        own_rows = own.value.reshape(half, rows)
        own_came = swap(own_rows, *over_grp[-1])
        gram_rows = put(own_rows, 0, 0)
        images = [product(gram_rows, whole, half, 0)]
        gram_rows = after(gram_rows, images[0])
        gram_rows = put_rung(rung_other, half, here)
        gram_rows = put_pair(half, jnp.logical_not(as_upper))
        gram_rows = put_came(came_first, here)
        gram_rows = put_came(came_second, there)
        gram_rows = put_rung(rung_second, half, there)
        own_came, gram_rows = lax.optimization_barrier((own_came, gram_rows))
        gram_rows = put(own_came, half, 0)
        images.append(product(gram_rows, whole, half, 1))

        def spread(image, *earlier):
            found = [image, on_chip(image)]
            for step in range(1, n_chip):
                got = from_chip(image, step)
                if earlier:
                    got = after(got, *earlier)
                found += [got, on_chip(got)]
            return found

        found_here = spread(images[0], images[1])
        side_there = 1 - side_here
        if half % 128 == 0:
            early = [*found_here, images[1], on_chip(images[1])]
            columns = [2 * slot + side_here for slot in slots]
            columns += [side_there, 2 + side_there, side_here]
            begun = add_terms(
                second_begin_kernel,
                gram_rows,
                jnp.stack(columns),
                early,
                (held, *images),
                jnp.float32,
            )
            late = []
            for step in range(1, n_chip):
                got = after(from_chip(images[1], step), begun)
                late += [got, on_chip(got)]
            columns = [2 * slot + side_there for slot in slots[2:]] + [side_here]
            return add_terms(
                second_end_kernel,
                gram_rows,
                jnp.stack(columns),
                late,
                (begun,),
                jnp.bfloat16,
                scratch=True,
                limit=58 << 20,
            )

        spread_image = in_order(spread(images[1]), there, in_order(found_here, here))
        second_image = jnp.dot(gram_rows, spread_image, preferred_element_type=jnp.float32)
        factor = 0.2 * math.sqrt(COLS)
        update = jnp.zeros(held.shape, jnp.bfloat16)
        for at, start in enumerate((here, there)):
            combined = (
                coef_linear * lax.dynamic_slice_in_dim(held, start, half, 0).astype(jnp.float32)
                + coef_cubic * images[at].astype(jnp.float32)
                + coef_quintic * second_image[at * half : (at + 1) * half]
            )
            update = lax.dynamic_update_slice_in_dim(
                update, (factor * combined).astype(jnp.bfloat16), start, 0
            )
        return update

    return body


def solution(mesh):
    sizes = mesh.shape
    in_specs = (P(("fsdp", "grp", "rep"), None),)
    out_specs = P("fsdp", ("grp", "rep"))
    body = make_body(sizes["fsdp"], sizes["grp"], sizes["rep"])
    return jax.shard_map(body, mesh=mesh, in_specs=in_specs, out_specs=out_specs, check_vma=False)
```
